256 devices in a mesh: tm: 16 (over z, core), rows: 16 (over y, x).
Axes of the slice: x: 4, y: 4, z: 8, core: 2. Of those that a mesh axis runs over, the one named last changes fastest.
Arguments:
- feats: bfloat16 [32, 32, 96, 640], P('tm', 'rows'), may hold values from -30 to 30, as said below
- norm_gain_vector: float32 [96], replicated, may hold values from 0.25 to 1.75
- conv_weight: bfloat16 [96, 2592], replicated, may hold values from -0.125 to 0.125
- out_gain: float32 [96], replicated, may hold values from 0.25 to 1.75
- rgb_weight: float32 [3, 96], replicated, may hold values from -0.625 to 0.625
- target: float32 [32, 32, 3, 640], P('tm', 'rows'), may hold values from -6 to 6
- pix_weight: float32 [32, 32, 3, 640], P('tm', 'rows'), may hold values from 0.5 to 60, as said below
- frame_seg: int32 [32], replicated, may hold values from 0 to 2, never falling along the last dimension, each value on 1 to 16 neighbouring positions
Outputs:
- grad_feats: bfloat16 [32, 32, 96, 640], P('tm', 'rows')
The draws below stay inside these ranges and needn't reach their ends.
Inputs may be any that keep to these rules, and one draw needn't show every extreme that they name: `feats`: finite values of order one to a few tens; their spread differs from frame to frame and row to row. `pix_weight`: positive weights. `frame_seg`: segments are runs of consecutive frames numbered from 0 upward.
All inputs are finite; a program needn't handle non-finite values.
Results may differ from the reference program's by a relative error of at most 0.0038.
Values may be sent and summed in bfloat16 or wider, within the bound.
A program may use at most 64 MiB of HBM per device.

```python
import math
import jax
import jax.numpy as jnp
import numpy as np
from jax import lax

C = 96
W = 640
TOTAL_FRAMES = 32
HEIGHT = 32


def draw_feats(key, part):
    key = jax.random.fold_in(key, 11)
    key_base, key_chan, key_shift = jax.random.split(key, 3)
    shape = (TOTAL_FRAMES, HEIGHT, C, W)
    frame_pos = jnp.arange(TOTAL_FRAMES, dtype=jnp.float32) / max(TOTAL_FRAMES - 1, 1)
    row_pos = jnp.arange(HEIGHT, dtype=jnp.float32) / max(HEIGHT - 1, 1)
    rising = (1.0 + frame_pos[:, None]) * (1.0 + row_pos[None, :])
    chan_scale = jnp.exp(1.15 * jax.random.uniform(key_chan, (C,), jnp.float32, -1.0, 1.0))
    base = jnp.clip(jax.random.normal(key_base, shape, jnp.float32), -4.0, 4.0)
    offset = 0.2 * jax.random.normal(key_shift, (C,), jnp.float32)
    pixel_values = 0.5 * base * rising[:, :, None, None] * chan_scale[None, None, :, None] + offset[None, None, :, None]
    return pixel_values.astype(jnp.bfloat16)


def draw_pix_weight(key, part):
    key = jax.random.fold_in(key, 23)
    key_base, key_level = jax.random.split(key, 2)
    shape = (TOTAL_FRAMES, HEIGHT, 3, W)
    frame_pos = jnp.arange(TOTAL_FRAMES, dtype=jnp.float32) / max(TOTAL_FRAMES - 1, 1)
    rising = 1.0 + 2.0 * frame_pos
    level = jnp.exp(jax.random.uniform(key_level, (TOTAL_FRAMES, HEIGHT), jnp.float32, 0.0, 2.3025))
    base = jnp.exp(jax.random.uniform(key_base, shape, jnp.float32, 0.0, 0.693))
    pixel_values = base * rising[:, None, None, None] * level[:, :, None, None]
    return pixel_values.astype(jnp.float32)


def block_scale(key, shape, shards, smallest, largest):
    def one(dim, blocks):
        steps = jax.random.uniform(jax.random.fold_in(jax.random.fold_in(key, 6), dim), (blocks,), jnp.float32, smallest / len(shards), largest / len(shards))
        return jnp.repeat(jnp.exp(steps), shape[dim] // blocks).reshape((-1,) + (1,) * (len(shape) - dim - 1))

    gain = one(*shards[0])
    for cut in shards[1:]:
        gain = gain * one(*cut)
    return gain


def length_profile(amount, total, reach, slope):
    weights = [(1 << 20) // math.isqrt(grade ** slope) + 1 for grade in range(2, amount + 1)]
    spare, counts = total - reach - (amount - 1), [1] * (amount - 1)
    while spare > 0:
        free = [i for i in range(amount - 1) if counts[i] < reach]
        whole, left = sum([weights[i] for i in free]), spare
        for i in free:
            more = min(reach - counts[i], max(1, left * weights[i] // whole), spare)
            counts[i] = counts[i] + more
            spare = spare - more
    return np.array([reach] + counts)


def ragged_sizes(own_key, number_of, total, limit, lean):
    if number_of == 2:
        one = jax.random.randint(own_key, (), max(1, total - limit), min(limit, total - 1) + 1)
        return jnp.stack([one, total - one])
    sizes = jnp.asarray(length_profile(number_of, total, limit, lean), jnp.int32)
    twos = (number_of - 1) // 2
    source_of, sink = sizes[1:1 + 2 * twos:2], sizes[2:2 + 2 * twos:2]
    room = jnp.minimum(source_of - 1, limit - sink)
    passed = jax.random.randint(jax.random.fold_in(own_key, 1), (twos,), 0, 1 << 20) % (room + 1)
    sizes = sizes.at[1:1 + 2 * twos:2].set(source_of - passed).at[2:2 + 2 * twos:2].set(sink + passed)
    return sizes[jax.random.permutation(jax.random.fold_in(own_key, 2), number_of)]


def scatter_about(key, extent, scale, most, pieces=(), kind=jnp.bfloat16):
    result = jax.random.normal(key, extent, jnp.float32) * scale
    if len(pieces) > 0:
        result = block_scale(key, extent, pieces, -0.22, 0.18) * result
    return jnp.clip(result, min=-most, max=most).astype(kind)


def setup_inputs(seed: int = 0) -> dict:
    key_list = jax.random.split(jax.random.key(seed), 9)
    feats = draw_feats(jax.random.fold_in(key_list[8], 71), 0)
    norm_gain_vector = jnp.clip(1.0 + 0.15 * jax.random.normal(key_list[1], (C,), jnp.float32), 0.25, 1.75)
    conv_weight = scatter_about(key_list[2], (C, 27 * C), (27 * C) ** -0.5, 0.125)
    out_gain = jnp.clip(1.0 + 0.15 * jax.random.normal(key_list[3], (C,), jnp.float32), 0.25, 1.75)
    rgb_weight = scatter_about(key_list[4], (3, C), C ** -0.5, 0.625, (), jnp.float32)
    target = scatter_about(key_list[5], (TOTAL_FRAMES, HEIGHT, 3, W), 1.0, 6.0, ((0, 16), (1, 16)), jnp.float32)
    pix_weight = draw_pix_weight(jax.random.fold_in(key_list[8], 71), 0)
    frame_seg = jnp.searchsorted(jnp.cumsum(ragged_sizes(key_list[7], 3, TOTAL_FRAMES, TOTAL_FRAMES // 2, 2)), jnp.arange(TOTAL_FRAMES), side="right").astype(jnp.int32)
    return dict(feats=feats, norm_gain_vector=norm_gain_vector, conv_weight=conv_weight, out_gain=out_gain, rgb_weight=rgb_weight, target=target, pix_weight=pix_weight, frame_seg=frame_seg)


EPS = 1e-06
DELTA = 1.0

def reference(feats, norm_gain_vector, conv_weight, out_gain, rgb_weight, target, pix_weight, frame_seg):
    frames, height, chans, width = feats.shape
    input_float = feats.astype(jnp.float32)
    inverse_std_dev = lax.rsqrt(lax.optimization_barrier(jnp.mean(input_float * input_float, axis=2, keepdims=True)) + EPS)
    normalized_input = input_float * inverse_std_dev
    scaled_normalized = normalized_input * norm_gain_vector[:, None]
    activated_input = jax.nn.silu(scaled_normalized).astype(jnp.bfloat16)
    minus = jnp.full((2,), -1, jnp.int32)
    seg_ext = jnp.concatenate([minus, frame_seg.astype(jnp.int32), minus])
    valid = jnp.stack([seg_ext[i:i + frames + 2] == seg_ext[2:frames + 4] for i in range(3)], 1).astype(jnp.float32)
    taps = conv_weight.astype(jnp.float32).reshape(chans, 27, chans)
    act_pad = jnp.pad(activated_input, ((2, 0), (1, 1), (0, 0), (1, 1)))

    def forward_frame(frame):
        total = jnp.zeros((height, chans, width), jnp.float32)
        for i in range(3):
            source = lax.dynamic_index_in_dim(act_pad, frame + i, 0, keepdims=False).astype(jnp.float32)
            part_sum = jnp.zeros((height, chans, width), jnp.float32)
            for j in range(3):
                for l in range(3):
                    piece = source[j:j + height, :, l:l + width]
                    part_sum = part_sum + jnp.einsum('oc,hcw->how', taps[:, (i * 3 + j) * 3 + l, :], piece)
            total = total + valid[frame, i] * part_sum
        return total
    conv_out = lax.map(forward_frame, jnp.arange(frames))
    y_full = input_float + conv_out
    out_rstd = lax.rsqrt(lax.optimization_barrier(jnp.mean(y_full * y_full, axis=2, keepdims=True)) + EPS)
    out_hat = y_full * out_rstd
    out_scaled = out_hat * out_gain[:, None]
    out_act = jax.nn.silu(out_scaled)
    rgb = jnp.einsum('ec,thcw->thew', rgb_weight, out_act, precision=lax.Precision.HIGHEST)
    weight_sum = jnp.sum(pix_weight)
    entries = frames * height * 3 * width
    g_rgb = pix_weight * jnp.clip(rgb - target, -DELTA, DELTA) * (entries / weight_sum)
    grad_act_out = jnp.einsum('ec,thew->thcw', rgb_weight, g_rgb, precision=lax.Precision.HIGHEST)
    out_sigma = jax.nn.sigmoid(out_scaled)
    out_term = grad_act_out * out_sigma * (1.0 + out_scaled * (1.0 - out_sigma)) * out_gain[:, None]
    out_proj = lax.optimization_barrier(jnp.mean(out_term * out_hat, axis=2, keepdims=True))
    output_gradient = out_rstd * (out_term - out_hat * out_proj)
    g_yb = output_gradient.astype(jnp.bfloat16)
    grad_pad = jnp.pad(g_yb, ((0, 2), (1, 1), (0, 0), (1, 1)))

    def adjoint_frame(frame):
        total = jnp.zeros((height, chans, width), jnp.float32)
        for i in range(3):
            later = frame + 2 - i
            source = lax.dynamic_index_in_dim(grad_pad, later, 0, keepdims=False).astype(jnp.float32)
            part_sum = jnp.zeros((height, chans, width), jnp.float32)
            for j in range(3):
                for l in range(3):
                    piece = source[2 - j:2 - j + height, :, 2 - l:2 - l + width]
                    part_sum = part_sum + jnp.einsum('oc,how->hcw', taps[:, (i * 3 + j) * 3 + l, :], piece)
            total = total + valid[later, i] * part_sum
        return total
    g_act = lax.map(adjoint_frame, jnp.arange(frames))
    sigma = jax.nn.sigmoid(scaled_normalized)
    correction_term = g_act * sigma * (1.0 + scaled_normalized * (1.0 - sigma)) * norm_gain_vector[:, None]
    projected_output = lax.optimization_barrier(jnp.mean(correction_term * normalized_input, axis=2, keepdims=True))
    input_gradient = output_gradient + inverse_std_dev * (correction_term - normalized_input * projected_output)
    return input_gradient.astype(jnp.bfloat16)
```

```python
import functools

import jax
import jax.numpy as jnp
from jax import lax
from jax.experimental import pallas as pl
from jax.experimental.pallas import tpu as pltpu
from jax.sharding import PartitionSpec as P

EPS = 1e-06
DELTA = 1.0
MESH = pl.DeviceIdType.MESH
F32 = jnp.float32
BF16 = jnp.bfloat16
L = 128
Z, UP, DOWN, TOP, BOT = range(5)
XT, XB = 5, 6


def kernel(
    n_tm, n_rows, n_x, n_chunks, chans,
    feats_hbm, gain_ref, w_hbm, og_ref, rgbw_ref, target_hbm, pix_hbm, seg_ref,
    out_hbm,
    fe, tgt, pix, wn, stack, wf, wb, prm, act, grad, dterm, rstd, gy, part, edge, obuf, wsum,
    lsem, osem, ssem, rsem, wssem, wrsem,
):
    t = lax.axis_index("tm")
    r = lax.axis_index("rows")
    tn, tp = lax.rem(t + 1, n_tm), lax.rem(t + n_tm - 1, n_tm)
    rn, rp = lax.rem(r + 1, n_rows), lax.rem(r + n_rows - 1, n_rows)
    n_y = n_rows // n_x
    x, y = lax.rem(r, n_x), r // n_x
    tl, th = lax.rem(t, 4), t // 4

    rounds = [
        [(t, y * n_x + lax.rem(x + k, n_x)) for k in range(1, n_x)],
        [(t, lax.rem(y + k, n_y) * n_x + x) for k in range(1, n_y)],
        [(th * 4 + lax.rem(tl + k, 4), r) for k in range(1, 4)],
        [(lax.rem(th + k, n_tm // 4) * 4 + tl, r) for k in range(1, n_tm // 4)],
    ]
    near = [(tn, r), (tp, r), (t, rn), (t, rp)]
    everyone = near + [d for group in rounds for d in group]
    bar = pltpu.get_barrier_semaphore()
    for d in everyone:
        pl.semaphore_signal(bar, inc=1, device_id=d, device_id_type=MESH)

    loads = [
        pltpu.make_async_copy(feats_hbm, fe, lsem.at[0]),
        pltpu.make_async_copy(pix_hbm, pix, lsem.at[1]),
        pltpu.make_async_copy(target_hbm, tgt, lsem.at[2]),
        pltpu.make_async_copy(w_hbm, wn, lsem.at[3]),
    ]
    for c in loads:
        c.start()

    for q, row in enumerate((gain_ref[...].reshape(1, chans), og_ref[...].reshape(1, chans), rgbw_ref[0:1, :], rgbw_ref[1:2, :], rgbw_ref[2:3, :])):
        prm[q] = jnp.broadcast_to(row, (L, chans)).T

    loads[1].wait()
    acc = jnp.zeros((1, L), F32)
    for f in range(2):
        for h in range(2):
            for k in range(n_chunks):
                acc = acc + jnp.sum(pix[f, h, :, k * L : (k + 1) * L], axis=0, keepdims=True)
    wsum[0, 0] = jnp.broadcast_to(acc, (8, L))

    loads[0].wait()
    for k in range(n_chunks):
        for f in range(2):
            for h in range(2):
                xf = fe[f, h, :, k * L : (k + 1) * L].astype(F32)
                rs = lax.rsqrt(jnp.mean(xf * xf, axis=0, keepdims=True) + EPS)
                xn = xf * rs * prm[0]
                sg = jax.nn.sigmoid(xn)
                act[k, 2 + f, 1 + h] = (xn * sg).astype(BF16)
                dterm[k, f, h] = sg * (1.0 + xn * (1.0 - sg)) * prm[0]
                rstd[k, f, h] = jnp.broadcast_to(rs, (8, L))

    pl.semaphore_wait(bar, len(everyone))

    even = lax.rem(t, 2) == 0
    odd = lax.rem(t, 2) == 1

    def remote(src, dst, ss, rs_, dev):
        return pltpu.make_async_remote_copy(
            src_ref=src, dst_ref=dst, send_sem=ss, recv_sem=rs_, device_id=dev, device_id_type=MESH
        )

    def copy(p, k, name):
        buf = act if p == 0 else grad
        own, oth = (pl.ds(2, 2), pl.ds(0, 2)) if p == 0 else (pl.ds(0, 2), pl.ds(2, 2))
        ahead = (tn, r) if p == 0 else (tp, r)
        up, down = (t, rp), (t, rn)
        src, dst, s, v, dev = dict(
            z=((own, pl.ds(1, 2)), (oth, pl.ds(1, 2)), Z, Z, ahead),
            up=((own, 1), (own, 3), UP, UP, up),
            down=((own, 2), (own, 0), DOWN, DOWN, down),
            xup=((oth, 1), (oth, 3), XB, BOT, up),
            xdown=((oth, 2), (oth, 0), XT, TOP, down),
            ttop=((own, 0), (oth, 0), TOP, TOP, ahead),
            tbot=((own, 3), (oth, 3), BOT, BOT, ahead),
        )[name]
        return remote(buf.at[(k, *src)], buf.at[(k, *dst)], ssem.at[p, k, s], rsem.at[p, k, v], dev)

    relays = (even, odd)

    def send(p, k):
        copy(p, k, "up").start()
        copy(p, k, "down").start()
        copy(p, k, "z").start()

    def relay_z(p, k):
        copy(p, k, "z").wait_recv()

        @pl.when(relays[p])
        def _():
            copy(p, k, "xup").start()
            copy(p, k, "xdown").start()

    def relay_rows(p, k):
        copy(p, k, "up").wait_recv()
        copy(p, k, "down").wait_recv()

        @pl.when(relays[p])
        def _():
            copy(p, k, "ttop").start()
            copy(p, k, "tbot").start()

    def corners(p, k):
        copy(p, k, "ttop").wait_recv()
        copy(p, k, "tbot").wait_recv()

    def sum_copies(q):
        return [
            remote(wsum.at[q, 0], wsum.at[q, k + 1], wssem.at[q, k], wrsem.at[q, k], d)
            for k, d in enumerate(rounds[q])
        ]

    def sum_start(q):
        for c in sum_copies(q):
            c.start()

    def sum_end(q):
        cs = sum_copies(q)
        for c in cs:
            c.wait_recv()
        wsum[q + 1, 0] = sum(wsum[q, k + 1] for k in range(len(cs))) + wsum[q, 0]

    for k in range(n_chunks):
        send(0, k)
    sum_start(0)

    loads[3].wait()
    kdim = 9 * chans
    lane = lax.broadcasted_iota(jnp.int32, (1, kdim), 1)
    first = [(lane >= a * 3 * chans) & (lane < a * 3 * chans + chans) for a in range(3)]
    last = [(lane >= (a * 3 + 2) * chans) & (lane < (a * 3 + 3) * chans) for a in range(3)]
    any_first = (first[0] | first[1]) | first[2]
    any_last = (last[0] | last[1]) | last[2]
    has_top = jnp.where(r > 0, 1.0, 0.0).astype(F32)
    has_bot = jnp.where(r < n_rows - 1, 1.0, 0.0).astype(F32)
    frames = 2 * n_tm
    seg = [seg_ref[lax.rem(2 * t + frames - 2 + q, frames)] for q in range(6)]
    has_before = jnp.where(t > 0, 1.0, 0.0).astype(F32)
    has_after = jnp.where(t < n_tm - 1, 1.0, 0.0).astype(F32)

    def same(a, b):
        return jnp.where(seg[a] == seg[b], 1.0, 0.0).astype(F32)

    def masks(near_, far_, backward):
        made = []
        for f in range(2):
            lo, mid, hi = (1.0, near_[f], far_[f]) if backward else (far_[f], near_[f], 1.0)
            byframe = jnp.where(lane < 3 * chans, lo, jnp.where(lane < 6 * chans, mid, hi))
            made.append(byframe * jnp.where(any_first, has_top, 1.0))
            made.append(byframe * jnp.where(any_last, has_bot, 1.0))
        return made

    for l in range(3):
        for ij in range(9):
            q = ij * 3 + l
            stack[l * chans : (l + 1) * chans, ij * chans : (ij + 1) * chans] = wn[:, q * chans : (q + 1) * chans]
    fm = masks((same(1, 2) * has_before, same(2, 3)), (same(0, 2) * has_before, same(1, 3) * has_before), False)
    for q in range(4):
        wf[q] = stack[...] * fm[q].astype(BF16)

    eye = (
        lax.broadcasted_iota(jnp.int32, (chans, chans), 0) == lax.broadcasted_iota(jnp.int32, (chans, chans), 1)
    ).astype(BF16)
    bm = masks((same(2, 3), same(3, 4) * has_after), (same(2, 4) * has_after, same(3, 5) * has_after), True)
    for m in range(3):
        rows_ = jnp.concatenate(
            [wn[:, ((8 - ab) * 3 + 2 - m) * chans : ((8 - ab) * 3 + 3 - m) * chans] for ab in range(9)], axis=0
        )
        turned = lax.dot_general(eye, rows_, (((1,), (1,)), ((), ())), preferred_element_type=F32).astype(BF16)
        for q in range(4):
            wb[q, m * chans : (m + 1) * chans, :] = turned * bm[q].astype(BF16)

    col = lax.broadcasted_iota(jnp.int32, (chans, L), 1)

    def conv(weights, buf, k, f, h, base):
        prod = jnp.dot(weights[f * 2 + h], buf[k, f : f + 3, h : h + 3].reshape(kdim, L), preferred_element_type=F32)
        right = pltpu.roll(prod[:chans], 1, axis=1)
        left = pltpu.roll(prod[2 * chans :], L - 1, axis=1)
        done = None
        if k > 0:
            done = part[f, h] + jnp.where(col == L - 1, left, 0.0)
            right_in = edge[f, h]
        else:
            right_in = jnp.zeros((chans, L), F32)
        new = prod[chans : 2 * chans] + jnp.where(col == 0, right_in, right) + jnp.where(col == L - 1, 0.0, left)
        if base is not None:
            new = new + base
        part[f, h] = new
        edge[f, h] = right
        return done

    def xfloat(k, f, h):
        return fe[f, h, :, k * L : (k + 1) * L].astype(F32)

    def middle(k, f, h, yy):
        og = prm[1]
        ys = lax.rsqrt(jnp.mean(yy * yy, axis=0, keepdims=True) + EPS)
        yh = yy * ys
        yn = yh * og
        sg = jax.nn.sigmoid(yn)
        zz = yn * sg
        gz = jnp.zeros((chans, L), F32)
        for e in range(3):
            rgb = jnp.sum(prm[2 + e] * zz, axis=0, keepdims=True)
            d = jnp.clip(rgb - tgt[f, h, e : e + 1, k * L : (k + 1) * L], -DELTA, DELTA)
            gz = gz + prm[2 + e] * (pix[f, h, e : e + 1, k * L : (k + 1) * L] * d)
        v = gz * sg * (1.0 + yn * (1.0 - sg)) * og
        vp = jnp.mean(v * yh, axis=0, keepdims=True)
        g = ys * (v - yh * vp)
        gy[k, f, h] = g
        grad[k, f, 1 + h] = g.astype(BF16)

    def final(k, f, h, ga, scale):
        rs = rstd[k, f, h, 0:1, :]
        xh = xfloat(k, f, h) * rs
        u = ga * dterm[k, f, h]
        pj = jnp.mean(u * xh, axis=0, keepdims=True)
        res = (gy[k, f, h] + rs * (u - xh * pj)) * scale
        obuf[f, h, :, k * L : (k + 1) * L] = res.astype(BF16)

    def store(k):
        return pltpu.make_async_copy(
            obuf.at[:, :, :, pl.ds(k * L, L)], out_hbm.at[:, :, :, pl.ds(k * L, L)], osem.at[k]
        )

    cells = [(f, h) for f in range(2) for h in range(2)]
    loads[2].wait()

    ahead = 2
    for k in range(min(ahead, n_chunks)):
        relay_rows(0, k)
        relay_z(0, k)
    for k in range(n_chunks):
        if k + ahead < n_chunks:
            relay_rows(0, k + ahead)
            relay_z(0, k + ahead)
        corners(0, k)
        for f, h in cells:
            done = conv(wf, act, k, f, h, xfloat(k, f, h))
            if k > 0:
                middle(k - 1, f, h, done)
        if k > 0:
            send(1, k - 1)
        if k < 3:
            sum_end(k)
            sum_start(k + 1)
        if k >= 3:
            relay_rows(1, k - 3)
            relay_z(1, k - 3)
    for f, h in cells:
        middle(n_chunks - 1, f, h, part[f, h])
    send(1, n_chunks - 1)
    sum_end(3)
    total = jnp.sum(wsum[4, 0, 0:1, :], axis=1, keepdims=True)
    scale = jnp.full((1, 1), 2.0 * n_tm * 2.0 * n_rows * 3.0 * n_chunks * L, F32) / total

    relayed = max(n_chunks - 3, 0)
    for k in range(n_chunks):
        while relayed < min(k + ahead + 1, n_chunks):
            relay_rows(1, relayed)
            relay_z(1, relayed)
            relayed += 1
        corners(1, k)
        for f, h in cells:
            done = conv(wb, grad, k, f, h, None)
            if k > 0:
                final(k - 1, f, h, done, scale)
        if k > 0:
            store(k - 1).start()
    for f, h in cells:
        final(n_chunks - 1, f, h, part[f, h], scale)
    store(n_chunks - 1).start()

    for p in range(2):
        for k in range(n_chunks):
            for name in ("up", "down", "z"):
                copy(p, k, name).wait_send()

            @pl.when(relays[p])
            def _():
                for name in ("xup", "xdown", "ttop", "tbot"):
                    copy(p, k, name).wait_send()

    for q in range(4):
        for c in sum_copies(q):
            c.wait_send()
    for k in range(n_chunks):
        store(k).wait()


def local(feats, gain, conv_weight, out_gain, rgb_weight, target, pix_weight, frame_seg):
    n_tm, n_rows = lax.axis_size("tm"), lax.axis_size("rows")
    frames, rows, chans, width = feats.shape
    nc = width // L
    hbm = pl.BlockSpec(memory_space=pl.ANY)
    vmem = pl.BlockSpec(memory_space=pltpu.VMEM)
    smem = pl.BlockSpec(memory_space=pltpu.SMEM)
    kd = 9 * chans
    return pl.pallas_call(
        functools.partial(kernel, n_tm, n_rows, 4, nc, chans),
        out_shape=jax.ShapeDtypeStruct(feats.shape, BF16),
        in_specs=[hbm, vmem, hbm, vmem, vmem, hbm, hbm, smem],
        out_specs=hbm,
        scratch_shapes=[
            pltpu.VMEM(feats.shape, BF16),
            pltpu.VMEM(target.shape, F32),
            pltpu.VMEM(pix_weight.shape, F32),
            pltpu.VMEM(conv_weight.shape, BF16),
            pltpu.VMEM((3 * chans, kd), BF16),
            pltpu.VMEM((4, 3 * chans, kd), BF16),
            pltpu.VMEM((4, 3 * chans, kd), BF16),
            pltpu.VMEM((5, chans, L), F32),
            pltpu.VMEM((nc, 4, 4, chans, L), BF16),
            pltpu.VMEM((nc, 4, 4, chans, L), BF16),
            pltpu.VMEM((nc, 2, 2, chans, L), F32),
            pltpu.VMEM((nc, 2, 2, 8, L), F32),
            pltpu.VMEM((nc, 2, 2, chans, L), F32),
            pltpu.VMEM((2, 2, chans, L), F32),
            pltpu.VMEM((2, 2, chans, L), F32),
            pltpu.VMEM(feats.shape, BF16),
            pltpu.VMEM((5, 4, 8, L), F32),
            pltpu.SemaphoreType.DMA((4,)),
            pltpu.SemaphoreType.DMA((nc,)),
            pltpu.SemaphoreType.DMA((2, nc, 7)),
            pltpu.SemaphoreType.DMA((2, nc, 5)),
            pltpu.SemaphoreType.DMA((4, 3)),
            pltpu.SemaphoreType.DMA((4, 3)),
        ],
        compiler_params=pltpu.CompilerParams(
            collective_id=0, has_side_effects=True, vmem_limit_bytes=56 * 1024 * 1024
        ),
    )(feats, gain, conv_weight, out_gain, rgb_weight, target, pix_weight, frame_seg)


def solution(mesh):
    placed = (
        P("tm", "rows", None, None),
        P(),
        P(),
        P(),
        P(),
        P("tm", "rows", None, None),
        P("tm", "rows", None, None),
        P(),
    )
    return jax.shard_map(
        local, mesh=mesh, in_specs=placed, out_specs=P("tm", "rows", None, None), check_vma=False
    )
```

```python
import functools

import jax
import jax.numpy as jnp
from jax import lax
from jax.experimental import pallas as pl
from jax.experimental.pallas import tpu as pltpu
from jax.sharding import PartitionSpec as P

EPS = 1e-06
DELTA = 1.0
MESH = pl.DeviceIdType.MESH
F32 = jnp.float32
BF16 = jnp.bfloat16
L = 128
Z, UP, DOWN = range(3)

def kernel(
    n_tm, n_rows, n_x, n_chunks, chans,
    feats_hbm, gain_ref, w_hbm, og_ref, rgbw_ref, target_hbm, pix_hbm, seg_ref,
    out_hbm,
    fe, tgt, pix, wn, mid_raw, out_raw, w_mid, w_out, prm, act, grad, dterm, rstd, gy, acc, part, edge, give, take, obuf, wsum, zsum,
    lsem, osem, ssem, rsem, wssem, wrsem, zssem, zrsem, hsem,
):
    t = lax.axis_index("tm")
    r = lax.axis_index("rows")
    n_y = n_rows // n_x
    x, y = lax.rem(r, n_x), r // n_x
    n_z = n_tm // 2
    not_first, not_last = t > 0, t < n_tm - 1
    has_up, has_down = r > 0, r < n_rows - 1

    group_x = [(t, y * n_x + lax.rem(x + k, n_x)) for k in range(1, n_x)]
    group_y = [(t, lax.rem(y + k, n_y) * n_x + x) for k in range(1, n_y)]
    mate = (t + 1 - 2 * lax.rem(t, 2), r)
    rounds = [group_x, group_y, [mate]]

    def along(d):
        return (t + 2 * d, r), (t + 2 * d >= 0 if d < 0 else t + 2 * d < n_tm)

    greet = [((t + 1, r), not_last), ((t - 1, r), not_first), ((t, r + 1), has_down), ((t, r - 1), has_up)]
    greet += [along(1), along(-1)] + [(d, None) for d in group_x + group_y]
    bar = pltpu.get_barrier_semaphore()

    def signal(sem, partners):
        for d, there in partners:
            if there is None:
                pl.semaphore_signal(sem, inc=1, device_id=d, device_id_type=MESH)
            else:

                @pl.when(there)
                def _():
                    pl.semaphore_signal(sem, inc=1, device_id=d, device_id_type=MESH)

    def await_all(sem, partners):
        amount = sum(1 if there is None else jnp.where(there, 1, 0) for _, there in partners)
        pl.semaphore_wait(sem, amount)

    signal(bar, greet)

    loads = [
        pltpu.make_async_copy(feats_hbm, fe, lsem.at[0]),
        pltpu.make_async_copy(pix_hbm, pix, lsem.at[1]),
        pltpu.make_async_copy(w_hbm, wn, lsem.at[3]),
        pltpu.make_async_copy(target_hbm, tgt, lsem.at[2]),
    ]
    for c in loads:
        c.start()

    @pl.when(jnp.logical_not(has_up))
    def _():
        take[:, :, 0] = jnp.zeros((2, n_chunks, 2, chans, L), BF16)

    @pl.when(jnp.logical_not(has_down))
    def _():
        take[:, :, 1] = jnp.zeros((2, n_chunks, 2, chans, L), BF16)

    @pl.when(jnp.logical_not(not_first))
    def _():
        act[:, 0:2] = jnp.zeros((n_chunks, 2, 2, chans, L), BF16)

    @pl.when(jnp.logical_not(not_last))
    def _():
        grad[:, 2:4] = jnp.zeros((n_chunks, 2, 2, chans, L), BF16)

    def column(row):
        return jnp.broadcast_to(row, (L, chans)).T

    prm[0] = column(gain_ref[...].reshape(1, chans))

    def remote(src, dst, ss, rs_, dev):
        return pltpu.make_async_remote_copy(
            src_ref=src, dst_ref=dst, send_sem=ss, recv_sem=rs_, device_id=dev, device_id_type=MESH
        )

    def copy(p, k, name):
        s, v = ssem.at[p, k], rsem.at[p, k]
        if name == Z:
            buf = (act if p == 0 else grad).at[k]
            own, oth = (pl.ds(2, 2), pl.ds(0, 2)) if p == 0 else (pl.ds(0, 2), pl.ds(2, 2))
            return remote(buf.at[own], buf.at[oth], s.at[Z], v.at[Z], (t + 1 - 2 * p, r))
        if name == UP:
            return remote(give.at[p, k, 0], take.at[p, k, 1], s.at[UP], v.at[UP], (t, r - 1))
        return remote(give.at[p, k, 1], take.at[p, k, 0], s.at[DOWN], v.at[DOWN], (t, r + 1))

    leaves = ({Z: not_last, UP: has_up, DOWN: has_down}, {Z: not_first, UP: has_up, DOWN: has_down})
    comes = ({Z: not_first, UP: has_down, DOWN: has_up}, {Z: not_last, UP: has_down, DOWN: has_up})

    def send(p, k, *names):
        for name in names:

            @pl.when(leaves[p][name])
            def _():
                copy(p, k, name).start()

    def receive(p, k, *names):
        for name in names:

            @pl.when(comes[p][name])
            def _():
                copy(p, k, name).wait_recv()

    def sum_copies(q):
        return [
            remote(wsum.at[q, 0], wsum.at[q, k + 1], wssem.at[q, k], wrsem.at[q, k], d)
            for k, d in enumerate(rounds[q])
        ]

    def sum_start(q):
        for c in sum_copies(q):
            c.start()

    def sum_end(q):
        cs = sum_copies(q)
        for c in cs:
            c.wait_recv()
        wsum[q + 1, 0] = sum(wsum[q, k + 1] for k in range(len(cs))) + wsum[q, 0]

    reach = [d for d in range(1 - n_z, n_z) if d != 0]

    def chip_copy(d):
        return remote(zsum.at[n_z - 1], zsum.at[n_z - 1 + d], zssem.at[n_z - 1 + d], zrsem.at[n_z - 1 + d], along(d)[0])

    def chips_start():
        zsum[n_z - 1] = wsum[3, 0]
        for d in reach:

            @pl.when(along(d)[1])
            def _():
                chip_copy(d).start()

    def chips_end():
        for d in reach:

            @pl.when(along(-d)[1])
            def _():
                chip_copy(d).wait_recv()

        everything = sum(zsum[q, 0:1, :] for q in range(2 * n_z - 1))
        total = jnp.sum(everything, axis=1, keepdims=True)
        return jnp.full((1, 1), 2.0 * n_tm * 2.0 * n_rows * 3.0 * n_chunks * L, F32) / total

    chain = [[along(1), along(-1)], [along(2), along(-2)], [along(4), along(-4)]]

    def hail(q):
        signal(hsem.at[q], chain[q])

    def hailed(q):
        await_all(hsem.at[q], chain[q])

    loads[0].wait()
    for k in range(n_chunks):
        for f in range(2):
            for h in range(2):
                xf = fe[f, h, :, k * L : (k + 1) * L].astype(F32)
                rs = lax.rsqrt(jnp.mean(xf * xf, axis=0, keepdims=True) + EPS)
                xn = xf * rs * prm[0]
                sg = jax.nn.sigmoid(xn)
                act[k, 2 + f, h] = (xn * sg).astype(BF16)
                dterm[k, f, h] = sg * (1.0 + xn * (1.0 - sg)) * prm[0]
                rstd[k, f, h] = jnp.broadcast_to(rs, (8, L))
        if k == 0:
            await_all(bar, greet)
        send(0, k, Z)

    loads[1].wait()
    weight = jnp.zeros((1, L), F32)
    for f in range(2):
        for e in range(3):
            for k in range(n_chunks):
                weight = weight + jnp.sum(pix[f, e, :, k * L : (k + 1) * L], axis=0, keepdims=True)
    wsum[0, 0] = jnp.broadcast_to(weight, (8, L))
    zsum[...] = jnp.zeros_like(zsum)
    sum_start(0)
    hail(0)
    for q, row in enumerate((og_ref[...].reshape(1, chans), rgbw_ref[0:1, :], rgbw_ref[1:2, :], rgbw_ref[2:3, :])):
        prm[1 + q] = column(row)

    loads[2].wait()
    tall = 3 * chans
    frames = 2 * n_tm
    seg = [seg_ref[lax.rem(2 * t + frames - 2 + q, frames)] for q in range(6)]

    def same(a, b):
        return jnp.where(seg[a] == seg[b], 1.0, 0.0).astype(F32)

    def mask(near_, far_, backward, rows_):
        lane = lax.broadcasted_iota(jnp.int32, (1, 3 * rows_ * chans), 1)
        lo, mid, hi = (1.0, near_, far_) if backward else (far_, near_, 1.0)
        return jnp.where(lane < rows_ * chans, lo, jnp.where(lane < 2 * rows_ * chans, mid, hi)).astype(BF16)

    def tap(q):
        return wn[:, q * chans : (q + 1) * chans]

    eye = (
        lax.broadcasted_iota(jnp.int32, (chans, chans), 0) == lax.broadcasted_iota(jnp.int32, (chans, chans), 1)
    ).astype(BF16)

    inner = [(0, (0, 1)), (1, (0, 1))]
    outer = [(-1, (0,)), (2, (1,))]

    def prepare(p):
        for part_of, raw, made in ((inner, mid_raw, w_mid), (outer, out_raw, w_out)):
            for n, (to, sources) in enumerate(part_of):
                for l in range(3):
                    at = n * tall + l * chans
                    if p == 0:
                        taps = [tap((i * 3 + h - to + 1) * 3 + l) for i in range(3) for h in sources]
                        for q, block in enumerate(taps):
                            raw[at : at + chans, q * chans : (q + 1) * chans] = block
                    else:
                        taps = [tap(((2 - a) * 3 + to + 1 - h) * 3 + 2 - l) for a in range(3) for h in sources]
                        raw[at : at + chans, :] = lax.dot_general(
                            eye, jnp.concatenate(taps, axis=0), (((1,), (1,)), ((), ())), preferred_element_type=F32
                        ).astype(BF16)
            for f in range(2):
                near_, far_ = (same(1 + f, 2 + f), same(f, 2 + f)) if p == 0 else (same(2 + f, 3 + f), same(2 + f, 4 + f))
                made[p, f] = raw[...] * mask(near_, far_, p == 1, len(part_of[0][1]))

    prepare(0)
    col = lax.broadcasted_iota(jnp.int32, (chans, L), 1)

    def shifted(prod, k, f, row):
        right = pltpu.roll(prod[:chans], 1, axis=1)
        left = pltpu.roll(prod[2 * chans :], L - 1, axis=1)
        done = None
        right_in = jnp.zeros((chans, L), F32)
        if k > 0:
            done = part[f, row] + jnp.where(col == L - 1, left, 0.0)
            right_in = edge[f, row]
        new = prod[chans : 2 * chans] + jnp.where(col == 0, right_in, right) + jnp.where(col == L - 1, 0.0, left)
        if k < n_chunks - 1:
            part[f, row] = new
            edge[f, row] = right
        return done, new

    def conv(p, k):
        buf = act if p == 0 else grad
        for f in range(2):
            both = jnp.dot(w_mid[p, f], buf[k, f : f + 3].reshape(2 * tall, L), preferred_element_type=F32)
            above = jnp.dot(
                w_out[p, f, :tall], buf[k, f : f + 3, 0].reshape(tall, L), preferred_element_type=F32
            )
            below = jnp.dot(
                w_out[p, f, tall:], buf[k, f : f + 3, 1].reshape(tall, L), preferred_element_type=F32
            )
            for row, prod in enumerate((above, both[:tall], both[tall:], below)):
                for q, value in zip((k - 1, k), shifted(prod, k, f, row)):
                    if value is None or (q == k and k < n_chunks - 1):
                        continue
                    if row in (1, 2):
                        acc[q, f, row - 1] = value
                    else:
                        give[p, q, row // 3, f] = value.astype(BF16)
        if k > 0:
            send(p, k - 1, UP, DOWN)
        if k == n_chunks - 1:
            send(p, k, UP, DOWN)

    def xfloat(k, f, h):
        return fe[f, h, :, k * L : (k + 1) * L].astype(F32)

    def middle(k, f, h):
        yy = xfloat(k, f, h) + acc[k, f, h] + take[0, k, h, f].astype(F32)
        og = prm[1]
        ys = lax.rsqrt(jnp.mean(yy * yy, axis=0, keepdims=True) + EPS)
        yh = yy * ys
        yn = yh * og
        sg = jax.nn.sigmoid(yn)
        zz = yn * sg
        gz = jnp.zeros((chans, L), F32)
        for e in range(3):
            rgb = jnp.sum(prm[2 + e] * zz, axis=0, keepdims=True)
            d = jnp.clip(rgb - tgt[f, e, h : h + 1, k * L : (k + 1) * L], -DELTA, DELTA)
            gz = gz + prm[2 + e] * (pix[f, e, h : h + 1, k * L : (k + 1) * L] * d)
        v = gz * sg * (1.0 + yn * (1.0 - sg)) * og
        vp = jnp.mean(v * yh, axis=0, keepdims=True)
        g = ys * (v - yh * vp)
        gy[k, f, h] = g
        grad[k, f, h] = g.astype(BF16)

    def final(k, f, h, scale):
        ga = acc[k, f, h] + take[1, k, h, f].astype(F32)
        rs = rstd[k, f, h, 0:1, :]
        xh = xfloat(k, f, h) * rs
        u = ga * dterm[k, f, h]
        pj = jnp.mean(u * xh, axis=0, keepdims=True)
        res = (gy[k, f, h] + rs * (u - xh * pj)) * scale
        obuf[f, h, :, k * L : (k + 1) * L] = res.astype(BF16)

    def store(k):
        return pltpu.make_async_copy(
            obuf.at[:, :, :, pl.ds(k * L, L)], out_hbm.at[:, :, :, pl.ds(k * L, L)], osem.at[k]
        )

    cells = [(f, h) for f in range(2) for h in range(2)]
    loads[3].wait()

    sum_end(0)
    sum_start(1)
    for k in range(n_chunks):
        receive(0, k, Z)
        conv(0, k)
        if k == 1:
            sum_end(1)
            sum_start(2)
        if k == 2:
            hailed(0)
            hail(1)
    sum_end(2)
    hailed(1)
    hail(2)
    prepare(1)
    for k in range(n_chunks):
        receive(0, k, UP, DOWN)
        for f, h in cells:
            middle(k, f, h)
        send(1, k, Z)
    hailed(2)
    chips_start()

    for k in range(n_chunks):
        receive(1, k, Z)
        conv(1, k)
    scale = chips_end()
    for k in range(n_chunks):
        receive(1, k, UP, DOWN)
        for f, h in cells:
            final(k, f, h, scale)
        store(k).start()

    for p in range(2):
        for name, there in leaves[p].items():

            @pl.when(there)
            def _():
                for k in range(n_chunks):
                    copy(p, k, name).wait_send()

    for q in range(3):
        for c in sum_copies(q):
            c.wait_send()
    for d in reach:

        @pl.when(along(d)[1])
        def _():
            chip_copy(d).wait_send()

    for k in range(n_chunks):
        store(k).wait()


def local(feats, gain, conv_weight, out_gain, rgb_weight, target, pix_weight, frame_seg):
    n_tm, n_rows = lax.axis_size("tm"), lax.axis_size("rows")
    frames, rows, chans, width = feats.shape
    nc = width // L
    hbm = pl.BlockSpec(memory_space=pl.ANY)
    vmem = pl.BlockSpec(memory_space=pltpu.VMEM)
    smem = pl.BlockSpec(memory_space=pltpu.SMEM)
    tall = 3 * chans
    return pl.pallas_call(
        functools.partial(kernel, n_tm, n_rows, 4, nc, chans),
        out_shape=jax.ShapeDtypeStruct(feats.shape, BF16),
        in_specs=[hbm, vmem, hbm, vmem, vmem, hbm, hbm, smem],
        out_specs=hbm,
        scratch_shapes=[
            pltpu.VMEM(feats.shape, BF16),
            pltpu.VMEM((frames, 3, rows, width), F32),
            pltpu.VMEM((frames, 3, rows, width), F32),
            pltpu.VMEM(conv_weight.shape, BF16),
            pltpu.VMEM((2 * tall, 2 * tall), BF16),
            pltpu.VMEM((2 * tall, tall), BF16),
            pltpu.VMEM((2, 2, 2 * tall, 2 * tall), BF16),
            pltpu.VMEM((2, 2, 2 * tall, tall), BF16),
            pltpu.VMEM((5, chans, L), F32),
            pltpu.VMEM((nc, 4, 2, chans, L), BF16),
            pltpu.VMEM((nc, 4, 2, chans, L), BF16),
            pltpu.VMEM((nc, 2, 2, chans, L), F32),
            pltpu.VMEM((nc, 2, 2, 8, L), F32),
            pltpu.VMEM((nc, 2, 2, chans, L), F32),
            pltpu.VMEM((nc, 2, 2, chans, L), F32),
            pltpu.VMEM((2, 4, chans, L), F32),
            pltpu.VMEM((2, 4, chans, L), F32),
            pltpu.VMEM((2, nc, 2, 2, chans, L), BF16),
            pltpu.VMEM((2, nc, 2, 2, chans, L), BF16),
            pltpu.VMEM(feats.shape, BF16),
            pltpu.VMEM((4, 4, 8, L), F32),
            pltpu.VMEM((n_tm - 1, 8, L), F32),
            pltpu.SemaphoreType.DMA((4,)),
            pltpu.SemaphoreType.DMA((nc,)),
            pltpu.SemaphoreType.DMA((2, nc, 3)),
            pltpu.SemaphoreType.DMA((2, nc, 3)),
            pltpu.SemaphoreType.DMA((3, 3)),
            pltpu.SemaphoreType.DMA((3, 3)),
            pltpu.SemaphoreType.DMA((n_tm - 1,)),
            pltpu.SemaphoreType.DMA((n_tm - 1,)),
            pltpu.SemaphoreType.REGULAR((3,)),
        ],
        compiler_params=pltpu.CompilerParams(
            collective_id=0, has_side_effects=True, vmem_limit_bytes=56 * 1024 * 1024
        ),
    )(
        feats, gain, conv_weight, out_gain, rgb_weight,
        target.transpose(0, 2, 1, 3), pix_weight.transpose(0, 2, 1, 3), frame_seg,
    )


def solution(mesh):
    placed = (
        P("tm", "rows", None, None),
        P(),
        P(),
        P(),
        P(),
        P("tm", "rows", None, None),
        P("tm", "rows", None, None),
        P(),
    )
    return jax.shard_map(
        local, mesh=mesh, in_specs=placed, out_specs=P("tm", "rows", None, None), check_vma=False
    )
```

```python
import functools

import jax
import jax.numpy as jnp
from jax import lax
from jax.experimental import pallas as pl
from jax.experimental.pallas import tpu as pltpu
from jax.sharding import PartitionSpec as P

EPS = 1e-06
DELTA = 1.0
MESH = pl.DeviceIdType.MESH
F32 = jnp.float32
BF16 = jnp.bfloat16
L = 128
Z, UP, DOWN = range(3)

def kernel(
    n_tm, n_rows, n_x, n_chunks, chans,
    feats_hbm, gain_hbm, w_hbm, og_hbm, rgbw_hbm, target_hbm, pix_hbm, seg_hbm,
    out_hbm,
    fe, gain_ref, og_ref, rgbw_ref, seg_ref, tgt, pix, wn, w_mid, w_out, rhs, prm, act, grad, dterm, rstd, gy, acc, part, edge, give, take, obuf, wsum, zsum,
    lsem, osem, ssem, rsem, wssem, wrsem, zssem, zrsem, hsem,
):
    t = lax.axis_index("tm")
    r = lax.axis_index("rows")
    n_y = n_rows // n_x
    x, y = lax.rem(r, n_x), r // n_x
    not_first, not_last = t > 0, t < n_tm - 1
    has_up, has_down = r > 0, r < n_rows - 1

    group_x = [(t, y * n_x + lax.rem(x + k, n_x)) for k in range(1, n_x)]
    group_y = [(t, lax.rem(y + k, n_y) * n_x + x) for k in range(1, n_y)]
    rounds = [group_x, group_y]

    def along(d):
        return (t + 2 * d, r), (t + 2 * d >= 0 if d < 0 else t + 2 * d < n_tm)

    greet = [((t + 1, r), not_last), ((t - 1, r), not_first), ((t, r + 1), has_down), ((t, r - 1), has_up)]
    greet += [along(1), along(-1)] + [(d, None) for d in group_x + group_y]
    bar = pltpu.get_barrier_semaphore()

    def signal(sem, partners):
        for d, there in partners:
            if there is None:
                pl.semaphore_signal(sem, inc=1, device_id=d, device_id_type=MESH)
            else:

                @pl.when(there)
                def _():
                    pl.semaphore_signal(sem, inc=1, device_id=d, device_id_type=MESH)

    def await_all(sem, partners):
        amount = sum(1 if there is None else jnp.where(there, 1, 0) for _, there in partners)
        pl.semaphore_wait(sem, amount)

    zsum[...] = jnp.zeros_like(zsum)
    signal(bar, greet)

    loads = {
        name: pltpu.make_async_copy(src, dst, lsem.at[q])
        for q, (name, src, dst) in enumerate((
            ("gain", gain_hbm, gain_ref),
            ("feats", feats_hbm, fe),
            ("pix", pix_hbm, pix),
            ("seg", seg_hbm, seg_ref),
            ("weights", w_hbm, wn),
            ("out_gain", og_hbm, og_ref),
            ("rgb", rgbw_hbm, rgbw_ref),
            ("target", target_hbm, tgt),
        ))
    }
    for c in loads.values():
        c.start()

    @pl.when(jnp.logical_not(has_up))
    def _():
        take[:, :, 0] = jnp.zeros((2, n_chunks, 2, chans, L), BF16)

    @pl.when(jnp.logical_not(has_down))
    def _():
        take[:, :, 1] = jnp.zeros((2, n_chunks, 2, chans, L), BF16)

    @pl.when(jnp.logical_not(not_first))
    def _():
        act[:, 0:2] = jnp.zeros((n_chunks, 2, 2, chans, L), BF16)

    @pl.when(jnp.logical_not(not_last))
    def _():
        grad[:, 2:4] = jnp.zeros((n_chunks, 2, 2, chans, L), BF16)

    def column(row):
        return jnp.broadcast_to(row, (L, chans)).T

    loads["gain"].wait()
    prm[0] = column(gain_ref[...].reshape(1, chans))

    def remote(src, dst, ss, rs_, dev):
        return pltpu.make_async_remote_copy(
            src_ref=src, dst_ref=dst, send_sem=ss, recv_sem=rs_, device_id=dev, device_id_type=MESH
        )

    def copy(p, k, name):
        s, v = ssem.at[p, k], rsem.at[p, k]
        if name == Z:
            buf = (act if p == 0 else grad).at[k]
            own, oth = (pl.ds(2, 2), pl.ds(0, 2)) if p == 0 else (pl.ds(0, 2), pl.ds(2, 2))
            return remote(buf.at[own], buf.at[oth], s.at[Z], v.at[Z], (t + 1 - 2 * p, r))
        if name == UP:
            return remote(give.at[p, k, 0], take.at[p, k, 1], s.at[UP], v.at[UP], (t, r - 1))
        return remote(give.at[p, k, 1], take.at[p, k, 0], s.at[DOWN], v.at[DOWN], (t, r + 1))

    leaves = ({Z: not_last, UP: has_up, DOWN: has_down}, {Z: not_first, UP: has_up, DOWN: has_down})
    comes = ({Z: not_first, UP: has_down, DOWN: has_up}, {Z: not_last, UP: has_down, DOWN: has_up})

    def send(p, k, *names):
        for name in names:

            @pl.when(leaves[p][name])
            def _():
                copy(p, k, name).start()

    def receive(p, k, *names):
        for name in names:

            @pl.when(comes[p][name])
            def _():
                copy(p, k, name).wait_recv()

    def sum_copies(q):
        return [
            remote(wsum.at[q, 0], wsum.at[q, k + 1], wssem.at[q, k], wrsem.at[q, k], d)
            for k, d in enumerate(rounds[q])
        ]

    def sum_start(q):
        for c in sum_copies(q):
            c.start()

    def sum_end(q):
        cs = sum_copies(q)
        for c in cs:
            c.wait_recv()
        wsum[q + 1, 0] = sum(wsum[q, k + 1] for k in range(len(cs))) + wsum[q, 0]

    reach = [d for d in range(1 - n_tm, n_tm) if d != 0]

    def on_tm(d):
        return t + d >= 0 if d < 0 else t + d < n_tm

    def plane_copy(d):
        q = n_tm - 1 + d
        return remote(zsum.at[n_tm - 1], zsum.at[q], zssem.at[q], zrsem.at[q], (t + d, r))

    def planes_start():
        zsum[n_tm - 1] = wsum[2, 0]
        for d in reach:

            @pl.when(on_tm(d))
            def _():
                plane_copy(d).start()

    def planes_end():
        for d in reach:

            @pl.when(on_tm(-d))
            def _():
                plane_copy(d).wait_recv()

        everything = sum(zsum[q, 0:1, :] for q in range(2 * n_tm - 1))
        total = jnp.sum(everything, axis=1, keepdims=True)
        return jnp.full((1, 1), 2.0 * n_tm * 2.0 * n_rows * 3.0 * n_chunks * L, F32) / total

    chain = [[along(1), along(-1)], [along(2), along(-2)], [along(4), along(-4)]]

    def hail(q):
        signal(hsem.at[q], chain[q])

    def hailed(q):
        await_all(hsem.at[q], chain[q])

    def weights_sum():
        loads["pix"].wait()
        weight = jnp.zeros((1, L), F32)
        for f in range(2):
            for e in range(3):
                for k in range(n_chunks):
                    weight = weight + jnp.sum(pix[f, e, :, k * L : (k + 1) * L], axis=0, keepdims=True)
        wsum[0, 0] = jnp.broadcast_to(weight, (8, L))

    loads["feats"].wait()
    for k in range(n_chunks):
        for f in range(2):
            for h in range(2):
                xf = fe[f, h, :, k * L : (k + 1) * L].astype(F32)
                rs = lax.rsqrt(jnp.mean(xf * xf, axis=0, keepdims=True) + EPS)
                xn = xf * rs * prm[0]
                sg = jax.nn.sigmoid(xn)
                act[k, 2 + f, h] = (xn * sg).astype(BF16)
                dterm[k, f, h] = sg * (1.0 + xn * (1.0 - sg)) * prm[0]
                rstd[k, f, h] = jnp.broadcast_to(rs, (8, L))
        if k == 0:
            await_all(bar, greet)
        send(0, k, Z)
        if k == 0:
            weights_sum()
            sum_start(0)
            hail(0)

    loads["weights"].wait()
    loads["seg"].wait()
    tall = 3 * chans
    frames = 2 * n_tm
    seg = [seg_ref[lax.rem(2 * t + frames - 2 + q, frames)] for q in range(6)]

    def same(a, b):
        return jnp.where(seg[a] == seg[b], 1.0, 0.0).astype(F32)

    def valid(p, f, i):
        if i == (2 if p == 0 else 0):
            return None
        a, b = (f + i, f + 2) if p == 0 else (2 + f, 2 + f + i)
        return jnp.full((1, L), same(a, b), F32).astype(BF16)

    checks = [[[valid(p, f, i) for i in range(3)] for f in range(2)] for p in range(2)]

    def tap(q):
        return wn[:, q * chans : (q + 1) * chans]

    eye = (
        lax.broadcasted_iota(jnp.int32, (chans, chans), 0) == lax.broadcasted_iota(jnp.int32, (chans, chans), 1)
    ).astype(BF16)

    inner = [(0, (0, 1)), (1, (0, 1))]
    outer = [(-1, (0,)), (2, (1,))]

    def prepare(p):
        for part_of, raw in ((inner, w_mid.at[p]), (outer, w_out.at[p])):
            for n, (to, sources) in enumerate(part_of):
                for l in range(3):
                    at = n * tall + l * chans
                    if p == 0:
                        taps = [tap((i * 3 + h - to + 1) * 3 + l) for i in range(3) for h in sources]
                        for q, block in enumerate(taps):
                            raw[at : at + chans, q * chans : (q + 1) * chans] = block
                    else:
                        taps = [tap(((2 - a) * 3 + to + 1 - h) * 3 + 2 - l) for a in range(3) for h in sources]
                        raw[at : at + chans, :] = lax.dot_general(
                            eye, jnp.concatenate(taps, axis=0), (((1,), (1,)), ((), ())), preferred_element_type=F32
                        ).astype(BF16)

    prepare(0)
    for name in ("out_gain", "rgb", "target"):
        loads[name].wait()
    for q, row in enumerate((og_ref[...].reshape(1, chans), rgbw_ref[0:1, :], rgbw_ref[1:2, :], rgbw_ref[2:3, :])):
        prm[1 + q] = column(row)
    col = lax.broadcasted_iota(jnp.int32, (chans, L), 1)

    def shifted(prod, k, f, row):
        right = pltpu.roll(prod[:chans], 1, axis=1)
        left = pltpu.roll(prod[2 * chans :], L - 1, axis=1)
        done = None
        right_in = jnp.zeros((chans, L), F32)
        if k > 0:
            done = part[f, row] + jnp.where(col == L - 1, left, 0.0)
            right_in = edge[f, row]
        new = prod[chans : 2 * chans] + jnp.where(col == 0, right_in, right) + jnp.where(col == L - 1, 0.0, left)
        if k < n_chunks - 1:
            part[f, row] = new
            edge[f, row] = right
        return done, new

    def conv(p, k):
        buf = act if p == 0 else grad
        for f in range(2):
            for i in range(3):
                block = buf[k, f + i]
                if checks[p][f][i] is not None:
                    block = block * checks[p][f][i]
                rhs[k, i, :, :, f * L : (f + 1) * L] = block
        both = jnp.dot(w_mid[p], rhs[k].reshape(2 * tall, 2 * L), preferred_element_type=F32)
        above = jnp.dot(w_out[p, :tall], rhs[k, :, 0].reshape(tall, 2 * L), preferred_element_type=F32)
        below = jnp.dot(w_out[p, tall:], rhs[k, :, 1].reshape(tall, 2 * L), preferred_element_type=F32)
        for row, prod in enumerate((above, both[:tall], both[tall:], below)):
            for f in range(2):
                for q, value in zip((k - 1, k), shifted(prod[:, f * L : (f + 1) * L], k, f, row)):
                    if value is None or (q == k and k < n_chunks - 1):
                        continue
                    if row in (1, 2):
                        acc[q, f, row - 1] = value
                    else:
                        give[p, q, row // 3, f] = value.astype(BF16)
        if k > 0:
            send(p, k - 1, UP, DOWN)
        if k == n_chunks - 1:
            send(p, k, UP, DOWN)

    def xfloat(k, f, h):
        return fe[f, h, :, k * L : (k + 1) * L].astype(F32)

    def middle(k, f, h):
        yy = xfloat(k, f, h) + acc[k, f, h] + take[0, k, h, f].astype(F32)
        og = prm[1]
        ys = lax.rsqrt(jnp.mean(yy * yy, axis=0, keepdims=True) + EPS)
        yh = yy * ys
        yn = yh * og
        sg = jax.nn.sigmoid(yn)
        zz = yn * sg
        gz = jnp.zeros((chans, L), F32)
        for e in range(3):
            rgb = jnp.sum(prm[2 + e] * zz, axis=0, keepdims=True)
            d = jnp.clip(rgb - tgt[f, e, h : h + 1, k * L : (k + 1) * L], -DELTA, DELTA)
            gz = gz + prm[2 + e] * (pix[f, e, h : h + 1, k * L : (k + 1) * L] * d)
        v = gz * sg * (1.0 + yn * (1.0 - sg)) * og
        vp = jnp.mean(v * yh, axis=0, keepdims=True)
        g = ys * (v - yh * vp)
        gy[k, f, h] = g
        grad[k, f, h] = g.astype(BF16)

    def final(k, f, h, scale):
        ga = acc[k, f, h] + take[1, k, h, f].astype(F32)
        rs = rstd[k, f, h, 0:1, :]
        xh = xfloat(k, f, h) * rs
        u = ga * dterm[k, f, h]
        pj = jnp.mean(u * xh, axis=0, keepdims=True)
        res = (gy[k, f, h] + rs * (u - xh * pj)) * scale
        obuf[f, h, :, k * L : (k + 1) * L] = res.astype(BF16)

    def store(k):
        return pltpu.make_async_copy(
            obuf.at[:, :, :, pl.ds(k * L, L)], out_hbm.at[:, :, :, pl.ds(k * L, L)], osem.at[k]
        )

    cells = [(f, h) for f in range(2) for h in range(2)]

    for k in range(n_chunks):
        receive(0, k, Z)
        conv(0, k)
        if k in (1, 3):
            hailed(k // 2)
            hail(k // 2 + 1)
        if k == 2:
            sum_end(0)
            sum_start(1)
    sum_end(1)

    late = t >= n_tm // 2

    @pl.when(late)
    def _():
        hailed(2)
        planes_start()

    prepare(1)
    for k in range(n_chunks):
        receive(0, k, UP, DOWN)
        for f, h in cells:
            middle(k, f, h)
        send(1, k, Z)

    @pl.when(jnp.logical_not(late))
    def _():
        hailed(2)
        planes_start()

    for k in range(n_chunks):
        receive(1, k, Z)
        conv(1, k)
    scale = planes_end()
    for k in range(n_chunks):
        receive(1, k, UP, DOWN)
        for f, h in cells:
            final(k, f, h, scale)
        store(k).start()

    for p in range(2):
        for name, there in leaves[p].items():

            @pl.when(there)
            def _():
                for k in range(n_chunks):
                    copy(p, k, name).wait_send()

    for q in range(2):
        for c in sum_copies(q):
            c.wait_send()
    for d in reach:

        @pl.when(on_tm(d))
        def _():
            plane_copy(d).wait_send()

    for k in range(n_chunks):
        store(k).wait()


def local(feats, gain, conv_weight, out_gain, rgb_weight, target, pix_weight, frame_seg):
    n_tm, n_rows = lax.axis_size("tm"), lax.axis_size("rows")
    frames, rows, chans, width = feats.shape
    nc = width // L
    hbm = pl.BlockSpec(memory_space=pltpu.HBM)
    tall = 3 * chans
    return pl.pallas_call(
        functools.partial(kernel, n_tm, n_rows, 4, nc, chans),
        out_shape=jax.ShapeDtypeStruct(feats.shape, BF16),
        in_specs=[hbm] * 8,
        out_specs=pl.BlockSpec(memory_space=pl.ANY),
        scratch_shapes=[
            pltpu.VMEM(feats.shape, BF16),
            pltpu.VMEM(gain.shape, F32),
            pltpu.VMEM(out_gain.shape, F32),
            pltpu.VMEM(rgb_weight.shape, F32),
            pltpu.SMEM(frame_seg.shape, jnp.int32),
            pltpu.VMEM((frames, 3, rows, width), F32),
            pltpu.VMEM((frames, 3, rows, width), F32),
            pltpu.VMEM(conv_weight.shape, BF16),
            pltpu.VMEM((2, 2 * tall, 2 * tall), BF16),
            pltpu.VMEM((2, 2 * tall, tall), BF16),
            pltpu.VMEM((nc, 3, rows, chans, 2 * L), BF16),
            pltpu.VMEM((5, chans, L), F32),
            pltpu.VMEM((nc, 4, 2, chans, L), BF16),
            pltpu.VMEM((nc, 4, 2, chans, L), BF16),
            pltpu.VMEM((nc, 2, 2, chans, L), F32),
            pltpu.VMEM((nc, 2, 2, 8, L), F32),
            pltpu.VMEM((nc, 2, 2, chans, L), F32),
            pltpu.VMEM((nc, 2, 2, chans, L), F32),
            pltpu.VMEM((2, 4, chans, L), F32),
            pltpu.VMEM((2, 4, chans, L), F32),
            pltpu.VMEM((2, nc, 2, 2, chans, L), BF16),
            pltpu.VMEM((2, nc, 2, 2, chans, L), BF16),
            pltpu.VMEM(feats.shape, BF16),
            pltpu.VMEM((3, 4, 8, L), F32),
            pltpu.VMEM((2 * n_tm - 1, 8, L), F32),
            pltpu.SemaphoreType.DMA((8,)),
            pltpu.SemaphoreType.DMA((nc,)),
            pltpu.SemaphoreType.DMA((2, nc, 3)),
            pltpu.SemaphoreType.DMA((2, nc, 3)),
            pltpu.SemaphoreType.DMA((2, 3)),
            pltpu.SemaphoreType.DMA((2, 3)),
            pltpu.SemaphoreType.DMA((2 * n_tm - 1,)),
            pltpu.SemaphoreType.DMA((2 * n_tm - 1,)),
            pltpu.SemaphoreType.REGULAR((3,)),
        ],
        compiler_params=pltpu.CompilerParams(
            collective_id=0, has_side_effects=True, vmem_limit_bytes=56 * 1024 * 1024
        ),
    )(
        feats, gain, conv_weight, out_gain, rgb_weight,
        target.transpose(0, 2, 1, 3), pix_weight.transpose(0, 2, 1, 3), frame_seg,
    )


def solution(mesh):
    placed = (
        P("tm", "rows", None, None),
        P(),
        P(),
        P(),
        P(),
        P("tm", "rows", None, None),
        P("tm", "rows", None, None),
        P(),
    )
    return jax.shard_map(
        local, mesh=mesh, in_specs=placed, out_specs=P("tm", "rows", None, None), check_vma=False
    )
```

```python
import functools

import jax
import jax.numpy as jnp
from jax import lax
from jax.experimental import pallas as pl
from jax.experimental.pallas import tpu as pltpu
from jax.sharding import PartitionSpec as P

EPS = 1e-06
DELTA = 1.0
MESH = pl.DeviceIdType.MESH
F32 = jnp.float32
BF16 = jnp.bfloat16
L = 128
Z, UP, DOWN = range(3)

def kernel(
    n_tm, n_rows, n_x, n_chunks, chans,
    feats_hbm, gain_hbm, w_hbm, og_hbm, rgbw_hbm, target_hbm, pix_hbm, seg_hbm,
    out_hbm,
    fe, gain_ref, og_ref, rgbw_ref, seg_ref, tgt, pix, wn, w_mid, w_out, rhs, prm, act, grad, dterm, rstd, gy, acc, part, edge, give, take, obuf, wsum, zsum,
    lsem, osem, ssem, rsem, wssem, wrsem, zssem, zrsem, hsem,
):
    t = lax.axis_index("tm")
    r = lax.axis_index("rows")
    n_y = n_rows // n_x
    x, y = lax.rem(r, n_x), r // n_x
    not_first, not_last = t > 0, t < n_tm - 1
    has_up, has_down = r > 0, r < n_rows - 1

    group_x = [(t, y * n_x + lax.rem(x + k, n_x)) for k in range(1, n_x)]
    group_y = [(t, lax.rem(y + k, n_y) * n_x + x) for k in range(1, n_y)]
    rounds = [group_x, group_y]

    def along(d):
        return (t + 2 * d, r), (t + 2 * d >= 0 if d < 0 else t + 2 * d < n_tm)

    greet = [((t + 1, r), not_last), ((t - 1, r), not_first), ((t, r + 1), has_down), ((t, r - 1), has_up)]
    greet += [along(1), along(-1)] + [(d, None) for d in group_x + group_y]
    bar = pltpu.get_barrier_semaphore()

    def signal(sem, partners):
        for d, there in partners:
            if there is None:
                pl.semaphore_signal(sem, inc=1, device_id=d, device_id_type=MESH)
            else:

                @pl.when(there)
                def _():
                    pl.semaphore_signal(sem, inc=1, device_id=d, device_id_type=MESH)

    def await_all(sem, partners):
        amount = sum(1 if there is None else jnp.where(there, 1, 0) for _, there in partners)
        pl.semaphore_wait(sem, amount)

    zsum[...] = jnp.zeros_like(zsum)
    signal(bar, greet)

    loads = {
        name: pltpu.make_async_copy(src, dst, lsem.at[q])
        for q, (name, src, dst) in enumerate((
            ("gain", gain_hbm, gain_ref),
            ("feats", feats_hbm, fe),
            ("pix", pix_hbm, pix),
            ("seg", seg_hbm, seg_ref),
            ("weights", w_hbm, wn),
            ("out_gain", og_hbm, og_ref),
            ("rgb", rgbw_hbm, rgbw_ref),
            ("target", target_hbm, tgt),
        ))
    }
    for c in loads.values():
        c.start()

    @pl.when(jnp.logical_not(has_up))
    def _():
        take[:, :, 0] = jnp.zeros((2, n_chunks, 2, chans, L), BF16)

    @pl.when(jnp.logical_not(has_down))
    def _():
        take[:, :, 1] = jnp.zeros((2, n_chunks, 2, chans, L), BF16)

    @pl.when(jnp.logical_not(not_first))
    def _():
        act[:, 0:2] = jnp.zeros((n_chunks, 2, 2, chans, L), BF16)

    @pl.when(jnp.logical_not(not_last))
    def _():
        grad[:, 2:4] = jnp.zeros((n_chunks, 2, 2, chans, L), BF16)

    def column(row):
        return jnp.broadcast_to(row, (L, chans)).T

    loads["gain"].wait()
    prm[0] = column(gain_ref[...].reshape(1, chans))

    def remote(src, dst, ss, rs_, dev):
        return pltpu.make_async_remote_copy(
            src_ref=src, dst_ref=dst, send_sem=ss, recv_sem=rs_, device_id=dev, device_id_type=MESH
        )

    def copy(p, k, name):
        s, v = ssem.at[p, k], rsem.at[p, k]
        if name == Z:
            buf = (act if p == 0 else grad).at[k]
            own, oth = (pl.ds(2, 2), pl.ds(0, 2)) if p == 0 else (pl.ds(0, 2), pl.ds(2, 2))
            return remote(buf.at[own], buf.at[oth], s.at[Z], v.at[Z], (t + 1 - 2 * p, r))
        if name == UP:
            return remote(give.at[p, k, 0], take.at[p, k, 1], s.at[UP], v.at[UP], (t, r - 1))
        return remote(give.at[p, k, 1], take.at[p, k, 0], s.at[DOWN], v.at[DOWN], (t, r + 1))

    leaves = ({Z: not_last, UP: has_up, DOWN: has_down}, {Z: not_first, UP: has_up, DOWN: has_down})
    comes = ({Z: not_first, UP: has_down, DOWN: has_up}, {Z: not_last, UP: has_down, DOWN: has_up})

    def send(p, k, *names):
        for name in names:

            @pl.when(leaves[p][name])
            def _():
                copy(p, k, name).start()

    def receive(p, k, *names):
        for name in names:

            @pl.when(comes[p][name])
            def _():
                copy(p, k, name).wait_recv()

    def sum_copies(q):
        return [
            remote(wsum.at[q, 0], wsum.at[q, k + 1], wssem.at[q, k], wrsem.at[q, k], d)
            for k, d in enumerate(rounds[q])
        ]

    def sum_start(q):
        for c in sum_copies(q):
            c.start()

    def sum_end(q):
        cs = sum_copies(q)
        for c in cs:
            c.wait_recv()
        wsum[q + 1, 0] = sum(wsum[q, k + 1] for k in range(len(cs))) + wsum[q, 0]

    reach = [d for d in range(1 - n_tm, n_tm) if d != 0]

    def on_tm(d):
        return t + d >= 0 if d < 0 else t + d < n_tm

    def plane_copy(d):
        q = n_tm - 1 + d
        return remote(zsum.at[n_tm - 1], zsum.at[q], zssem.at[q], zrsem.at[q], (t + d, r))

    def planes_start():
        zsum[n_tm - 1] = wsum[2, 0]
        for d in reach:

            @pl.when(on_tm(d))
            def _():
                plane_copy(d).start()

    def planes_end():
        for d in reach:

            @pl.when(on_tm(-d))
            def _():
                plane_copy(d).wait_recv()

        everything = sum(zsum[q, 0:1, :] for q in range(2 * n_tm - 1))
        total = jnp.sum(everything, axis=1, keepdims=True)
        return jnp.full((1, 1), 2.0 * n_tm * 2.0 * n_rows * 3.0 * n_chunks * L, F32) / total

    chain = [[along(1), along(-1)], [along(2), along(-2)], [along(4), along(-4)]]

    def hail(q):
        signal(hsem.at[q], chain[q])

    def hailed(q):
        await_all(hsem.at[q], chain[q])

    def weights_sum():
        loads["pix"].wait()
        weight = jnp.zeros((1, L), F32)
        for f in range(2):
            for e in range(3):
                for k in range(n_chunks):
                    weight = weight + jnp.sum(pix[f, e, :, k * L : (k + 1) * L], axis=0, keepdims=True)
        wsum[0, 0] = jnp.broadcast_to(weight, (8, L))

    loads["feats"].wait()
    for k in range(n_chunks):
        for f in range(2):
            for h in range(2):
                xf = fe[f, h, :, k * L : (k + 1) * L].astype(F32)
                rs = lax.rsqrt(jnp.mean(xf * xf, axis=0, keepdims=True) + EPS)
                xn = xf * rs * prm[0]
                sg = jax.nn.sigmoid(xn)
                act[k, 2 + f, h] = (xn * sg).astype(BF16)
                dterm[k, f, h] = sg * (1.0 + xn * (1.0 - sg)) * prm[0]
                rstd[k, f, h] = jnp.broadcast_to(rs, (8, L))
        if k == 0:
            await_all(bar, greet)
        send(0, k, Z)
        if k == 0:
            weights_sum()
            sum_start(0)
            hail(0)

    loads["weights"].wait()
    loads["seg"].wait()
    tall = 3 * chans
    frames = 2 * n_tm
    seg = [seg_ref[lax.rem(2 * t + frames - 2 + q, frames)] for q in range(6)]

    def same(a, b):
        return jnp.where(seg[a] == seg[b], 1.0, 0.0).astype(F32)

    def valid(p, f, i):
        if i == (2 if p == 0 else 0):
            return None
        a, b = (f + i, f + 2) if p == 0 else (2 + f, 2 + f + i)
        return jnp.full((1, L), same(a, b), F32).astype(BF16)

    checks = [[[valid(p, f, i) for i in range(3)] for f in range(2)] for p in range(2)]

    def tap(q):
        return wn[:, q * chans : (q + 1) * chans]

    eye = (
        lax.broadcasted_iota(jnp.int32, (chans, chans), 0) == lax.broadcasted_iota(jnp.int32, (chans, chans), 1)
    ).astype(BF16)

    inner = [(0, (0, 1)), (1, (0, 1))]
    outer = [(-1, (0,)), (2, (1,))]

    def prepare(p):
        for part_of, raw in ((inner, w_mid.at[p]), (outer, w_out.at[p])):
            for n, (to, sources) in enumerate(part_of):
                for l in range(3):
                    at = n * tall + l * chans
                    if p == 0:
                        taps = [tap((i * 3 + h - to + 1) * 3 + l) for i in range(3) for h in sources]
                        for q, block in enumerate(taps):
                            raw[at : at + chans, q * chans : (q + 1) * chans] = block
                    else:
                        taps = [tap(((2 - a) * 3 + to + 1 - h) * 3 + 2 - l) for a in range(3) for h in sources]
                        raw[at : at + chans, :] = lax.dot_general(
                            eye, jnp.concatenate(taps, axis=0), (((1,), (1,)), ((), ())), preferred_element_type=F32
                        ).astype(BF16)

    prepare(0)
    for name in ("out_gain", "rgb", "target"):
        loads[name].wait()
    for q, row in enumerate((og_ref[...].reshape(1, chans), rgbw_ref[0:1, :], rgbw_ref[1:2, :], rgbw_ref[2:3, :])):
        prm[1 + q] = column(row)
    col = lax.broadcasted_iota(jnp.int32, (chans, L), 1)

    def shifted(prod, k, f, row):
        right = pltpu.roll(prod[:chans], 1, axis=1)
        left = pltpu.roll(prod[2 * chans :], L - 1, axis=1)
        done = None
        right_in = jnp.zeros((chans, L), F32)
        if k > 0:
            done = part[f, row] + jnp.where(col == L - 1, left, 0.0)
            right_in = edge[f, row]
        new = prod[chans : 2 * chans] + jnp.where(col == 0, right_in, right) + jnp.where(col == L - 1, 0.0, left)
        if k < n_chunks - 1:
            part[f, row] = new
            edge[f, row] = right
        return done, new

    def conv(p, k):
        buf = act if p == 0 else grad
        for f in range(2):
            for i in range(3):
                block = buf[k, f + i]
                if checks[p][f][i] is not None:
                    block = block * checks[p][f][i]
                rhs[k, i, :, :, f * L : (f + 1) * L] = block
        both = jnp.dot(w_mid[p], rhs[k].reshape(2 * tall, 2 * L), preferred_element_type=F32)
        above = jnp.dot(w_out[p, :tall], rhs[k, :, 0].reshape(tall, 2 * L), preferred_element_type=F32)
        below = jnp.dot(w_out[p, tall:], rhs[k, :, 1].reshape(tall, 2 * L), preferred_element_type=F32)
        for row, prod in enumerate((above, both[:tall], both[tall:], below)):
            for f in range(2):
                for q, value in zip((k - 1, k), shifted(prod[:, f * L : (f + 1) * L], k, f, row)):
                    if value is None or (q == k and k < n_chunks - 1):
                        continue
                    if row in (1, 2):
                        acc[q, f, row - 1] = value
                    else:
                        give[p, q, row // 3, f] = value.astype(BF16)
        if k > 0:
            send(p, k - 1, UP, DOWN)
        if k == n_chunks - 1:
            send(p, k, UP, DOWN)

    def xfloat(k, f, h):
        return fe[f, h, :, k * L : (k + 1) * L].astype(F32)

    def middle(k, f, h):
        yy = xfloat(k, f, h) + acc[k, f, h] + take[0, k, h, f].astype(F32)
        og = prm[1]
        ys = lax.rsqrt(jnp.mean(yy * yy, axis=0, keepdims=True) + EPS)
        yh = yy * ys
        yn = yh * og
        sg = jax.nn.sigmoid(yn)
        zz = yn * sg
        gz = jnp.zeros((chans, L), F32)
        for e in range(3):
            rgb = jnp.sum(prm[2 + e] * zz, axis=0, keepdims=True)
            d = jnp.clip(rgb - tgt[f, e, h : h + 1, k * L : (k + 1) * L], -DELTA, DELTA)
            gz = gz + prm[2 + e] * (pix[f, e, h : h + 1, k * L : (k + 1) * L] * d)
        v = gz * sg * (1.0 + yn * (1.0 - sg)) * og
        vp = jnp.mean(v * yh, axis=0, keepdims=True)
        g = ys * (v - yh * vp)
        gy[k, f, h] = g
        grad[k, f, h] = g.astype(BF16)

    def final(k, f, h, scale):
        ga = acc[k, f, h] + take[1, k, h, f].astype(F32)
        rs = rstd[k, f, h, 0:1, :]
        xh = xfloat(k, f, h) * rs
        u = ga * dterm[k, f, h]
        pj = jnp.mean(u * xh, axis=0, keepdims=True)
        res = (gy[k, f, h] + rs * (u - xh * pj)) * scale
        obuf[f, h, :, k * L : (k + 1) * L] = res.astype(BF16)

    def store(k):
        return pltpu.make_async_copy(
            obuf.at[:, :, :, pl.ds(k * L, L)], out_hbm.at[:, :, :, pl.ds(k * L, L)], osem.at[k]
        )

    cells = [(f, h) for f in range(2) for h in range(2)]

    for k in range(n_chunks):
        receive(0, k, Z)
        conv(0, k)
        if k in (1, 3):
            hailed(k // 2)
            hail(k // 2 + 1)
        if k == 3:
            sum_end(0)
            sum_start(1)

    prepare(1)
    for k in range(n_chunks):
        receive(0, k, UP, DOWN)
        for f, h in cells:
            middle(k, f, h)
        send(1, k, Z)

    sum_end(1)
    hailed(2)
    planes_start()

    for k in range(n_chunks):
        receive(1, k, Z)
        conv(1, k)
    scale = planes_end()
    for k in range(n_chunks):
        receive(1, k, UP, DOWN)
        for f, h in cells:
            final(k, f, h, scale)
        store(k).start()

    for p in range(2):
        for name, there in leaves[p].items():

            @pl.when(there)
            def _():
                for k in range(n_chunks):
                    copy(p, k, name).wait_send()

    for q in range(2):
        for c in sum_copies(q):
            c.wait_send()
    for d in reach:

        @pl.when(on_tm(d))
        def _():
            plane_copy(d).wait_send()

    for k in range(n_chunks):
        store(k).wait()


def local(feats, gain, conv_weight, out_gain, rgb_weight, target, pix_weight, frame_seg):
    n_tm, n_rows = lax.axis_size("tm"), lax.axis_size("rows")
    frames, rows, chans, width = feats.shape
    nc = width // L
    hbm = pl.BlockSpec(memory_space=pltpu.HBM)
    tall = 3 * chans
    return pl.pallas_call(
        functools.partial(kernel, n_tm, n_rows, 4, nc, chans),
        out_shape=pltpu.VMEM(feats.shape, BF16),
        in_specs=[hbm] * 8,
        out_specs=pl.BlockSpec(memory_space=pl.ANY),
        scratch_shapes=[
            pltpu.VMEM(feats.shape, BF16),
            pltpu.VMEM(gain.shape, F32),
            pltpu.VMEM(out_gain.shape, F32),
            pltpu.VMEM(rgb_weight.shape, F32),
            pltpu.SMEM(frame_seg.shape, jnp.int32),
            pltpu.VMEM((frames, 3, rows, width), F32),
            pltpu.VMEM((frames, 3, rows, width), F32),
            pltpu.VMEM(conv_weight.shape, BF16),
            pltpu.VMEM((2, 2 * tall, 2 * tall), BF16),
            pltpu.VMEM((2, 2 * tall, tall), BF16),
            pltpu.VMEM((nc, 3, rows, chans, 2 * L), BF16),
            pltpu.VMEM((5, chans, L), F32),
            pltpu.VMEM((nc, 4, 2, chans, L), BF16),
            pltpu.VMEM((nc, 4, 2, chans, L), BF16),
            pltpu.VMEM((nc, 2, 2, chans, L), F32),
            pltpu.VMEM((nc, 2, 2, 8, L), F32),
            pltpu.VMEM((nc, 2, 2, chans, L), F32),
            pltpu.VMEM((nc, 2, 2, chans, L), F32),
            pltpu.VMEM((2, 4, chans, L), F32),
            pltpu.VMEM((2, 4, chans, L), F32),
            pltpu.VMEM((2, nc, 2, 2, chans, L), BF16),
            pltpu.VMEM((2, nc, 2, 2, chans, L), BF16),
            pltpu.VMEM(feats.shape, BF16),
            pltpu.VMEM((3, 4, 8, L), F32),
            pltpu.VMEM((2 * n_tm - 1, 8, L), F32),
            pltpu.SemaphoreType.DMA((8,)),
            pltpu.SemaphoreType.DMA((nc,)),
            pltpu.SemaphoreType.DMA((2, nc, 3)),
            pltpu.SemaphoreType.DMA((2, nc, 3)),
            pltpu.SemaphoreType.DMA((2, 3)),
            pltpu.SemaphoreType.DMA((2, 3)),
            pltpu.SemaphoreType.DMA((2 * n_tm - 1,)),
            pltpu.SemaphoreType.DMA((2 * n_tm - 1,)),
            pltpu.SemaphoreType.REGULAR((3,)),
        ],
        compiler_params=pltpu.CompilerParams(
            collective_id=0, has_side_effects=True, vmem_limit_bytes=56 * 1024 * 1024
        ),
    )(
        feats, gain, conv_weight, out_gain, rgb_weight,
        target.transpose(0, 2, 1, 3), pix_weight.transpose(0, 2, 1, 3), frame_seg,
    )


def solution(mesh):
    placed = (
        P("tm", "rows", None, None),
        P(),
        P(),
        P(),
        P(),
        P("tm", "rows", None, None),
        P("tm", "rows", None, None),
        P(),
    )
    return jax.shard_map(
        local, mesh=mesh, in_specs=placed, out_specs=P("tm", "rows", None, None), check_vma=False
    )
```

```python
import functools

import jax
import jax.numpy as jnp
from jax import lax
from jax.experimental import pallas as pl
from jax.experimental.pallas import tpu as pltpu
from jax.sharding import PartitionSpec as P

EPS = 1e-06
DELTA = 1.0
MESH = pl.DeviceIdType.MESH
F32 = jnp.float32
BF16 = jnp.bfloat16
L = 128
Z, UP, DOWN = range(3)

def kernel(
    n_tm, n_rows, n_x, n_chunks, chans,
    feats_hbm, gain_hbm, w_hbm, og_hbm, rgbw_hbm, target_hbm, pix_hbm, seg_hbm,
    out_hbm,
    fe, gain_ref, og_ref, rgbw_ref, seg_ref, tgt, pix, wn, w_mid, w_out, rhs, prm, act, grad, dterm, rstd, gy, acc, part, edge, give, take, obuf, wsum, zsum,
    lsem, osem, ssem, rsem, wssem, wrsem, zssem, zrsem, hsem,
):
    t = lax.axis_index("tm")
    r = lax.axis_index("rows")
    n_y = n_rows // n_x
    x, y = lax.rem(r, n_x), r // n_x
    not_first, not_last = t > 0, t < n_tm - 1
    has_up, has_down = r > 0, r < n_rows - 1

    group_x = [(t, y * n_x + lax.rem(x + k, n_x)) for k in range(1, n_x)]
    group_y = [(t, lax.rem(y + k, n_y) * n_x + x) for k in range(1, n_y)]
    rounds = [group_x, group_y]

    def along(d):
        return (t + 2 * d, r), (t + 2 * d >= 0 if d < 0 else t + 2 * d < n_tm)

    greet = [((t + 1, r), not_last), ((t - 1, r), not_first), ((t, r + 1), has_down), ((t, r - 1), has_up)]
    greet += [along(1), along(-1)] + [(d, None) for d in group_x + group_y]
    bar = pltpu.get_barrier_semaphore()

    def signal(sem, partners):
        for d, there in partners:
            if there is None:
                pl.semaphore_signal(sem, inc=1, device_id=d, device_id_type=MESH)
            else:

                @pl.when(there)
                def _():
                    pl.semaphore_signal(sem, inc=1, device_id=d, device_id_type=MESH)

    def await_all(sem, partners):
        amount = sum(1 if there is None else jnp.where(there, 1, 0) for _, there in partners)
        pl.semaphore_wait(sem, amount)

    zsum[...] = jnp.zeros_like(zsum)
    signal(bar, greet)

    loads = {
        name: pltpu.make_async_copy(src, dst, lsem.at[q])
        for q, (name, src, dst) in enumerate((
            ("gain", gain_hbm, gain_ref),
            ("feats", feats_hbm, fe),
            ("pix", pix_hbm, pix),
            ("seg", seg_hbm, seg_ref),
            ("weights", w_hbm, wn),
            ("out_gain", og_hbm, og_ref),
            ("rgb", rgbw_hbm, rgbw_ref),
            ("target", target_hbm, tgt),
        ))
    }
    for c in loads.values():
        c.start()

    @pl.when(jnp.logical_not(has_up))
    def _():
        take[:, :, 0] = jnp.zeros((2, n_chunks, 2, chans, L), BF16)

    @pl.when(jnp.logical_not(has_down))
    def _():
        take[:, :, 1] = jnp.zeros((2, n_chunks, 2, chans, L), BF16)

    @pl.when(jnp.logical_not(not_first))
    def _():
        act[:, 0:2] = jnp.zeros((n_chunks, 2, 2, chans, L), BF16)

    @pl.when(jnp.logical_not(not_last))
    def _():
        grad[:, 2:4] = jnp.zeros((n_chunks, 2, 2, chans, L), BF16)

    def column(row):
        return jnp.broadcast_to(row, (L, chans)).T

    loads["gain"].wait()
    prm[0] = column(gain_ref[...].reshape(1, chans))

    def remote(src, dst, ss, rs_, dev):
        return pltpu.make_async_remote_copy(
            src_ref=src, dst_ref=dst, send_sem=ss, recv_sem=rs_, device_id=dev, device_id_type=MESH
        )

    def copy(p, k, name):
        s, v = ssem.at[p, k], rsem.at[p, k]
        if name == Z:
            buf = (act if p == 0 else grad).at[k]
            own, oth = (pl.ds(2, 2), pl.ds(0, 2)) if p == 0 else (pl.ds(0, 2), pl.ds(2, 2))
            return remote(buf.at[own], buf.at[oth], s.at[Z], v.at[Z], (lax.rem(t + n_tm + 1 - 2 * p, n_tm), r))
        if name == UP:
            return remote(give.at[p, k, 0], take.at[p, k, 1], s.at[UP], v.at[UP], (t, lax.rem(r + n_rows - 1, n_rows)))
        return remote(give.at[p, k, 1], take.at[p, k, 0], s.at[DOWN], v.at[DOWN], (t, lax.rem(r + 1, n_rows)))

    leaves = ({Z: not_last, UP: has_up, DOWN: has_down}, {Z: not_first, UP: has_up, DOWN: has_down})
    comes = ({Z: not_first, UP: has_down, DOWN: has_up}, {Z: not_last, UP: has_down, DOWN: has_up})

    def send(p, k, *names):
        for name in names:

            @pl.when(leaves[p][name])
            def _():
                copy(p, k, name).start()

    def receive(p, k, *names):
        for name in names:

            @pl.when(comes[p][name])
            def _():
                copy(p, k, name).wait_recv()

    def sum_copies(q):
        return [
            remote(wsum.at[q, 0], wsum.at[q, k + 1], wssem.at[q, k], wrsem.at[q, k], d)
            for k, d in enumerate(rounds[q])
        ]

    def sum_start(q):
        for c in sum_copies(q):
            c.start()

    def sum_end(q):
        cs = sum_copies(q)
        for c in cs:
            c.wait_recv()
        wsum[q + 1, 0] = sum(wsum[q, k + 1] for k in range(len(cs))) + wsum[q, 0]

    reach = [d for d in range(1 - n_tm, n_tm) if d != 0]

    def on_tm(d):
        return t + d >= 0 if d < 0 else t + d < n_tm

    def plane_copy(d):
        q = n_tm - 1 + d
        return remote(zsum.at[n_tm - 1], zsum.at[q], zssem.at[q], zrsem.at[q], (lax.rem(t + n_tm + d, n_tm), r))

    def planes_start():
        zsum[n_tm - 1] = wsum[2, 0]
        for d in reach:

            @pl.when(on_tm(d))
            def _():
                plane_copy(d).start()

    def planes_end():
        for d in reach:

            @pl.when(on_tm(-d))
            def _():
                plane_copy(d).wait_recv()

        everything = sum(zsum[q, 0:1, :] for q in range(2 * n_tm - 1))
        total = jnp.sum(everything, axis=1, keepdims=True)
        return jnp.full((1, 1), 2.0 * n_tm * 2.0 * n_rows * 3.0 * n_chunks * L, F32) / total

    chain = [[along(1), along(-1)], [along(2), along(-2)], [along(4), along(-4)]]

    def hail(q):
        signal(hsem.at[q], chain[q])

    def hailed(q):
        await_all(hsem.at[q], chain[q])

    def weights_sum():
        loads["pix"].wait()
        weight = jnp.zeros((1, L), F32)
        for f in range(2):
            for e in range(3):
                for k in range(n_chunks):
                    weight = weight + jnp.sum(pix[f, e, :, k * L : (k + 1) * L], axis=0, keepdims=True)
        wsum[0, 0] = jnp.broadcast_to(weight, (8, L))

    loads["feats"].wait()
    for k in range(n_chunks):
        for f in range(2):
            for h in range(2):
                xf = fe[f, h, :, k * L : (k + 1) * L].astype(F32)
                rs = lax.rsqrt(jnp.mean(xf * xf, axis=0, keepdims=True) + EPS)
                xn = xf * rs * prm[0]
                sg = jax.nn.sigmoid(xn)
                act[k, 2 + f, h] = (xn * sg).astype(BF16)
                dterm[k, f, h] = sg * (1.0 + xn * (1.0 - sg)) * prm[0]
                rstd[k, f, h] = jnp.broadcast_to(rs, (8, L))
        if k == 0:
            await_all(bar, greet)
        send(0, k, Z)
        if k == 0:
            weights_sum()
            sum_start(0)
            hail(0)

    loads["weights"].wait()
    loads["seg"].wait()
    tall = 3 * chans
    frames = 2 * n_tm
    seg = [seg_ref[lax.rem(2 * t + frames - 2 + q, frames)] for q in range(6)]

    def same(a, b):
        return jnp.where(seg[a] == seg[b], 1.0, 0.0).astype(F32)

    def valid(p, f, i):
        if i == (2 if p == 0 else 0):
            return None
        a, b = (f + i, f + 2) if p == 0 else (2 + f, 2 + f + i)
        return jnp.full((1, L), same(a, b), F32).astype(BF16)

    checks = [[[valid(p, f, i) for i in range(3)] for f in range(2)] for p in range(2)]

    def tap(q):
        return wn[:, q * chans : (q + 1) * chans]

    eye = (
        lax.broadcasted_iota(jnp.int32, (chans, chans), 0) == lax.broadcasted_iota(jnp.int32, (chans, chans), 1)
    ).astype(BF16)

    inner = [(0, (0, 1)), (1, (0, 1))]
    outer = [(-1, (0,)), (2, (1,))]

    def prepare(p):
        for part_of, raw in ((inner, w_mid.at[p]), (outer, w_out.at[p])):
            for n, (to, sources) in enumerate(part_of):
                for l in range(3):
                    at = n * tall + l * chans
                    if p == 0:
                        taps = [tap((i * 3 + h - to + 1) * 3 + l) for i in range(3) for h in sources]
                        for q, block in enumerate(taps):
                            raw[at : at + chans, q * chans : (q + 1) * chans] = block
                    else:
                        taps = [tap(((2 - a) * 3 + to + 1 - h) * 3 + 2 - l) for a in range(3) for h in sources]
                        raw[at : at + chans, :] = lax.dot_general(
                            eye, jnp.concatenate(taps, axis=0), (((1,), (1,)), ((), ())), preferred_element_type=F32
                        ).astype(BF16)

    prepare(0)
    for name in ("out_gain", "rgb", "target"):
        loads[name].wait()
    for q, row in enumerate((og_ref[...].reshape(1, chans), rgbw_ref[0:1, :], rgbw_ref[1:2, :], rgbw_ref[2:3, :])):
        prm[1 + q] = column(row)
    col = lax.broadcasted_iota(jnp.int32, (chans, L), 1)

    def shifted(prod, k, f, row):
        right = pltpu.roll(prod[:chans], 1, axis=1)
        left = pltpu.roll(prod[2 * chans :], L - 1, axis=1)
        done = None
        right_in = jnp.zeros((chans, L), F32)
        if k > 0:
            done = part[f, row] + jnp.where(col == L - 1, left, 0.0)
            right_in = edge[f, row]
        new = prod[chans : 2 * chans] + jnp.where(col == 0, right_in, right) + jnp.where(col == L - 1, 0.0, left)
        if k < n_chunks - 1:
            part[f, row] = new
            edge[f, row] = right
        return done, new

    def conv(p, k):
        buf = act if p == 0 else grad
        for f in range(2):
            for i in range(3):
                block = buf[k, f + i]
                if checks[p][f][i] is not None:
                    block = block * checks[p][f][i]
                rhs[k, i, :, :, f * L : (f + 1) * L] = block
        both = jnp.dot(w_mid[p], rhs[k].reshape(2 * tall, 2 * L), preferred_element_type=F32)
        above = jnp.dot(w_out[p, :tall], rhs[k, :, 0].reshape(tall, 2 * L), preferred_element_type=F32)
        below = jnp.dot(w_out[p, tall:], rhs[k, :, 1].reshape(tall, 2 * L), preferred_element_type=F32)
        for row, prod in enumerate((above, both[:tall], both[tall:], below)):
            for f in range(2):
                for q, value in zip((k - 1, k), shifted(prod[:, f * L : (f + 1) * L], k, f, row)):
                    if value is None or (q == k and k < n_chunks - 1):
                        continue
                    if row in (1, 2):
                        acc[q, f, row - 1] = value
                    else:
                        give[p, q, row // 3, f] = value.astype(BF16)
        if k > 0:
            send(p, k - 1, UP, DOWN)
        if k == n_chunks - 1:
            send(p, k, UP, DOWN)

    def xfloat(k, f, h):
        return fe[f, h, :, k * L : (k + 1) * L].astype(F32)

    def middle(k, f, h):
        yy = xfloat(k, f, h) + acc[k, f, h] + take[0, k, h, f].astype(F32)
        og = prm[1]
        ys = lax.rsqrt(jnp.mean(yy * yy, axis=0, keepdims=True) + EPS)
        yh = yy * ys
        yn = yh * og
        sg = jax.nn.sigmoid(yn)
        zz = yn * sg
        gz = jnp.zeros((chans, L), F32)
        for e in range(3):
            rgb = jnp.sum(prm[2 + e] * zz, axis=0, keepdims=True)
            d = jnp.clip(rgb - tgt[f, e, h : h + 1, k * L : (k + 1) * L], -DELTA, DELTA)
            gz = gz + prm[2 + e] * (pix[f, e, h : h + 1, k * L : (k + 1) * L] * d)
        v = gz * sg * (1.0 + yn * (1.0 - sg)) * og
        vp = jnp.mean(v * yh, axis=0, keepdims=True)
        g = ys * (v - yh * vp)
        gy[k, f, h] = g
        grad[k, f, h] = g.astype(BF16)

    def final(k, f, h, scale):
        ga = acc[k, f, h] + take[1, k, h, f].astype(F32)
        rs = rstd[k, f, h, 0:1, :]
        xh = xfloat(k, f, h) * rs
        u = ga * dterm[k, f, h]
        pj = jnp.mean(u * xh, axis=0, keepdims=True)
        res = (gy[k, f, h] + rs * (u - xh * pj)) * scale
        obuf[f, h, :, k * L : (k + 1) * L] = res.astype(BF16)

    def store(k):
        return pltpu.make_async_copy(
            obuf.at[:, :, :, pl.ds(k * L, L)], out_hbm.at[:, :, :, pl.ds(k * L, L)], osem.at[k]
        )

    cells = [(f, h) for f in range(2) for h in range(2)]

    for k in range(n_chunks):
        receive(0, k, Z)
        conv(0, k)
        if k in (1, 3):
            hailed(k // 2)
            hail(k // 2 + 1)
        if k == 3:
            sum_end(0)
            sum_start(1)

    prepare(1)
    for k in range(n_chunks):
        receive(0, k, UP, DOWN)
        for f, h in cells:
            middle(k, f, h)
        send(1, k, Z)

    sum_end(1)
    hailed(2)
    planes_start()

    for k in range(n_chunks):
        receive(1, k, Z)
        conv(1, k)
    scale = planes_end()
    for k in range(n_chunks):
        receive(1, k, UP, DOWN)
        for f, h in cells:
            final(k, f, h, scale)
        store(k).start()

    for p in range(2):
        for name, there in leaves[p].items():

            @pl.when(there)
            def _():
                for k in range(n_chunks):
                    copy(p, k, name).wait_send()

    for q in range(2):
        for c in sum_copies(q):
            c.wait_send()
    for d in reach:

        @pl.when(on_tm(d))
        def _():
            plane_copy(d).wait_send()

    for k in range(n_chunks):
        store(k).wait()


def local(feats, gain, conv_weight, out_gain, rgb_weight, target, pix_weight, frame_seg):
    n_tm, n_rows = lax.axis_size("tm"), lax.axis_size("rows")
    frames, rows, chans, width = feats.shape
    nc = width // L
    hbm = pl.BlockSpec(memory_space=pltpu.HBM)
    tall = 3 * chans
    return pl.pallas_call(
        functools.partial(kernel, n_tm, n_rows, 4, nc, chans),
        out_shape=pltpu.VMEM(feats.shape, BF16),
        in_specs=[hbm] * 8,
        out_specs=pl.BlockSpec(memory_space=pl.ANY),
        scratch_shapes=[
            pltpu.VMEM(feats.shape, BF16),
            pltpu.VMEM(gain.shape, F32),
            pltpu.VMEM(out_gain.shape, F32),
            pltpu.VMEM(rgb_weight.shape, F32),
            pltpu.SMEM(frame_seg.shape, jnp.int32),
            pltpu.VMEM((frames, 3, rows, width), F32),
            pltpu.VMEM((frames, 3, rows, width), F32),
            pltpu.VMEM(conv_weight.shape, BF16),
            pltpu.VMEM((2, 2 * tall, 2 * tall), BF16),
            pltpu.VMEM((2, 2 * tall, tall), BF16),
            pltpu.VMEM((nc, 3, rows, chans, 2 * L), BF16),
            pltpu.VMEM((5, chans, L), F32),
            pltpu.VMEM((nc, 4, 2, chans, L), BF16),
            pltpu.VMEM((nc, 4, 2, chans, L), BF16),
            pltpu.VMEM((nc, 2, 2, chans, L), F32),
            pltpu.VMEM((nc, 2, 2, 8, L), F32),
            pltpu.VMEM((nc, 2, 2, chans, L), F32),
            pltpu.VMEM((nc, 2, 2, chans, L), F32),
            pltpu.VMEM((2, 4, chans, L), F32),
            pltpu.VMEM((2, 4, chans, L), F32),
            pltpu.VMEM((2, nc, 2, 2, chans, L), BF16),
            pltpu.VMEM((2, nc, 2, 2, chans, L), BF16),
            pltpu.VMEM(feats.shape, BF16),
            pltpu.VMEM((3, 4, 8, L), F32),
            pltpu.VMEM((2 * n_tm - 1, 8, L), F32),
            pltpu.SemaphoreType.DMA((8,)),
            pltpu.SemaphoreType.DMA((nc,)),
            pltpu.SemaphoreType.DMA((2, nc, 3)),
            pltpu.SemaphoreType.DMA((2, nc, 3)),
            pltpu.SemaphoreType.DMA((2, 3)),
            pltpu.SemaphoreType.DMA((2, 3)),
            pltpu.SemaphoreType.DMA((2 * n_tm - 1,)),
            pltpu.SemaphoreType.DMA((2 * n_tm - 1,)),
            pltpu.SemaphoreType.REGULAR((3,)),
        ],
        compiler_params=pltpu.CompilerParams(
            collective_id=0, has_side_effects=True, vmem_limit_bytes=56 * 1024 * 1024
        ),
    )(
        feats, gain, conv_weight, out_gain, rgb_weight,
        target.transpose(0, 2, 1, 3), pix_weight.transpose(0, 2, 1, 3), frame_seg,
    )


def solution(mesh):
    placed = (
        P("tm", "rows", None, None),
        P(),
        P(),
        P(),
        P(),
        P("tm", "rows", None, None),
        P("tm", "rows", None, None),
        P(),
    )
    return jax.shard_map(
        local, mesh=mesh, in_specs=placed, out_specs=P("tm", "rows", None, None), check_vma=False
    )
```

```python
import functools

import jax
import jax.numpy as jnp
from jax import lax
from jax.experimental import pallas as pl
from jax.experimental.pallas import tpu as pltpu
from jax.sharding import PartitionSpec as P

EPS = 1e-06
DELTA = 1.0
MESH = pl.DeviceIdType.MESH
F32 = jnp.float32
BF16 = jnp.bfloat16
L = 128
Z, UP, DOWN = range(3)

def kernel(
    n_tm, n_rows, n_x, n_chunks, chans,
    feats_hbm, gain_hbm, w_hbm, og_hbm, rgbw_hbm, target_hbm, pix_hbm, seg_hbm,
    out_hbm,
    fe, gain_ref, og_ref, rgbw_ref, seg_ref, tgt, pix, wn, w_mid, w_out, rhs, prm, act, grad, dterm, rstd, gy, acc, part, edge, give, take, obuf, wsum, zsum,
    lsem, osem, ssem, rsem, wssem, wrsem, zssem, zrsem, hsem,
):
    t = lax.axis_index("tm")
    r = lax.axis_index("rows")
    n_y = n_rows // n_x
    x, y = lax.rem(r, n_x), r // n_x
    not_first, not_last = t > 0, t < n_tm - 1
    has_up, has_down = r > 0, r < n_rows - 1

    group_x = [(t, y * n_x + lax.rem(x + k, n_x)) for k in range(1, n_x)]
    group_y = [(t, lax.rem(y + k, n_y) * n_x + x) for k in range(1, n_y)]
    rounds = [group_x, group_y]

    def along(d):
        return (t + 2 * d, r), (t + 2 * d >= 0 if d < 0 else t + 2 * d < n_tm)

    greet = [((t + 1, r), not_last), ((t - 1, r), not_first), ((t, r + 1), has_down), ((t, r - 1), has_up)]
    greet += [along(1), along(-1)] + [(d, None) for d in group_x + group_y]
    bar = pltpu.get_barrier_semaphore()

    def signal(sem, partners):
        for d, there in partners:
            if there is None:
                pl.semaphore_signal(sem, inc=1, device_id=d, device_id_type=MESH)
            else:

                @pl.when(there)
                def _():
                    pl.semaphore_signal(sem, inc=1, device_id=d, device_id_type=MESH)

    def await_all(sem, partners):
        amount = sum(1 if there is None else jnp.where(there, 1, 0) for _, there in partners)
        pl.semaphore_wait(sem, amount)

    zsum[...] = jnp.zeros_like(zsum)
    signal(bar, greet)

    loads = {
        name: pltpu.make_async_copy(src, dst, lsem.at[q])
        for q, (name, src, dst) in enumerate((
            ("gain", gain_hbm, gain_ref),
            ("feats", feats_hbm, fe),
            ("pix", pix_hbm, pix),
            ("seg", seg_hbm, seg_ref),
            ("weights", w_hbm, wn),
            ("out_gain", og_hbm, og_ref),
            ("rgb", rgbw_hbm, rgbw_ref),
            ("target", target_hbm, tgt),
        ))
    }
    for c in loads.values():
        c.start()

    @pl.when(jnp.logical_not(has_up))
    def _():
        take[:, :, 0] = jnp.zeros((2, n_chunks, 2, chans, L), BF16)

    @pl.when(jnp.logical_not(has_down))
    def _():
        take[:, :, 1] = jnp.zeros((2, n_chunks, 2, chans, L), BF16)

    @pl.when(jnp.logical_not(not_first))
    def _():
        act[:, 0:2] = jnp.zeros((n_chunks, 2, 2, chans, L), BF16)

    @pl.when(jnp.logical_not(not_last))
    def _():
        grad[:, 2:4] = jnp.zeros((n_chunks, 2, 2, chans, L), BF16)

    def column(row):
        return jnp.broadcast_to(row, (L, chans)).T

    loads["gain"].wait()
    prm[0] = column(gain_ref[...].reshape(1, chans))

    def remote(src, dst, ss, rs_, dev):
        return pltpu.make_async_remote_copy(
            src_ref=src, dst_ref=dst, send_sem=ss, recv_sem=rs_, device_id=dev, device_id_type=MESH
        )

    def copy(p, k, name):
        s, v = ssem.at[p, k], rsem.at[p, k]
        if name == Z:
            buf = (act if p == 0 else grad).at[k]
            own, oth = (pl.ds(2, 2), pl.ds(0, 2)) if p == 0 else (pl.ds(0, 2), pl.ds(2, 2))
            return remote(buf.at[own], buf.at[oth], s.at[Z], v.at[Z], (lax.rem(t + n_tm + 1 - 2 * p, n_tm), r))
        if name == UP:
            return remote(give.at[p, k, 0], take.at[p, k, 1], s.at[UP], v.at[UP], (t, lax.rem(r + n_rows - 1, n_rows)))
        return remote(give.at[p, k, 1], take.at[p, k, 0], s.at[DOWN], v.at[DOWN], (t, lax.rem(r + 1, n_rows)))

    leaves = ({Z: not_last, UP: has_up, DOWN: has_down}, {Z: not_first, UP: has_up, DOWN: has_down})
    comes = ({Z: not_first, UP: has_down, DOWN: has_up}, {Z: not_last, UP: has_down, DOWN: has_up})

    def send(p, k, *names):
        for name in names:

            @pl.when(leaves[p][name])
            def _():
                copy(p, k, name).start()

    def receive(p, k, *names):
        for name in names:

            @pl.when(comes[p][name])
            def _():
                copy(p, k, name).wait_recv()

    def sum_copies(q):
        return [
            remote(wsum.at[q, 0], wsum.at[q, k + 1], wssem.at[q, k], wrsem.at[q, k], d)
            for k, d in enumerate(rounds[q])
        ]

    def sum_start(q):
        for c in sum_copies(q):
            c.start()

    def sum_end(q):
        cs = sum_copies(q)
        for c in cs:
            c.wait_recv()
        wsum[q + 1, 0] = sum(wsum[q, k + 1] for k in range(len(cs))) + wsum[q, 0]

    reach = [d for d in range(1 - n_tm, n_tm) if d != 0]

    def on_tm(d):
        return t + d >= 0 if d < 0 else t + d < n_tm

    def plane_copy(d):
        q = n_tm - 1 + d
        return remote(zsum.at[n_tm - 1], zsum.at[q], zssem.at[q], zrsem.at[q], (lax.rem(t + n_tm + d, n_tm), r))

    def planes_start():
        zsum[n_tm - 1] = wsum[2, 0]
        for d in reach:

            @pl.when(on_tm(d))
            def _():
                plane_copy(d).start()

    def planes_end():
        for d in reach:

            @pl.when(on_tm(-d))
            def _():
                plane_copy(d).wait_recv()

        everything = sum(zsum[q, 0:1, :] for q in range(2 * n_tm - 1))
        total = jnp.sum(everything, axis=1, keepdims=True)
        return jnp.full((1, 1), 2.0 * n_tm * 2.0 * n_rows * 3.0 * n_chunks * L, F32) / total

    chain = [[along(1), along(-1)], [along(2), along(-2)], [along(4), along(-4)]]

    def hail(q):
        signal(hsem.at[q], chain[q])

    def hailed(q):
        await_all(hsem.at[q], chain[q])

    def weights_sum():
        loads["pix"].wait()
        weight = jnp.zeros((1, L), F32)
        for f in range(2):
            for e in range(3):
                for k in range(n_chunks):
                    weight = weight + jnp.sum(pix[f, e, :, k * L : (k + 1) * L], axis=0, keepdims=True)
        wsum[0, 0] = weight

    loads["feats"].wait()
    for k in range(n_chunks):
        for f in range(2):
            for h in range(2):
                xf = fe[f, h, :, k * L : (k + 1) * L].astype(F32)
                rs = lax.rsqrt(jnp.mean(xf * xf, axis=0, keepdims=True) + EPS)
                xn = xf * rs * prm[0]
                sg = jax.nn.sigmoid(xn)
                act[k, 2 + f, h] = (xn * sg).astype(BF16)
                dterm[k, f, h] = sg * (1.0 + xn * (1.0 - sg)) * prm[0]
                rstd[k, f, h] = jnp.broadcast_to(rs, (8, L))
        if k == 0:
            await_all(bar, greet)
        send(0, k, Z)
        if k == 0:
            weights_sum()
            sum_start(0)
            hail(0)

    loads["weights"].wait()
    loads["seg"].wait()
    tall = 3 * chans
    frames = 2 * n_tm
    seg = [seg_ref[lax.rem(2 * t + frames - 2 + q, frames)] for q in range(6)]

    def same(a, b):
        return jnp.where(seg[a] == seg[b], 1.0, 0.0).astype(F32)

    def valid(p, f, i):
        if i == (2 if p == 0 else 0):
            return None
        a, b = (f + i, f + 2) if p == 0 else (2 + f, 2 + f + i)
        return jnp.full((1, L), same(a, b), F32).astype(BF16)

    checks = [[[valid(p, f, i) for i in range(3)] for f in range(2)] for p in range(2)]

    def tap(q):
        return wn[:, q * chans : (q + 1) * chans]

    eye = (
        lax.broadcasted_iota(jnp.int32, (chans, chans), 0) == lax.broadcasted_iota(jnp.int32, (chans, chans), 1)
    ).astype(BF16)

    inner = [(0, (0, 1)), (1, (0, 1))]
    outer = [(-1, (0,)), (2, (1,))]

    def prepare(p):
        for part_of, raw in ((inner, w_mid.at[p]), (outer, w_out.at[p])):
            for n, (to, sources) in enumerate(part_of):
                for l in range(3):
                    at = n * tall + l * chans
                    if p == 0:
                        taps = [tap((i * 3 + h - to + 1) * 3 + l) for i in range(3) for h in sources]
                        for q, block in enumerate(taps):
                            raw[at : at + chans, q * chans : (q + 1) * chans] = block
                    else:
                        taps = [tap(((2 - a) * 3 + to + 1 - h) * 3 + 2 - l) for a in range(3) for h in sources]
                        raw[at : at + chans, :] = lax.dot_general(
                            eye, jnp.concatenate(taps, axis=0), (((1,), (1,)), ((), ())), preferred_element_type=F32
                        ).astype(BF16)

    prepare(0)
    for name in ("out_gain", "rgb", "target"):
        loads[name].wait()
    for q, row in enumerate((og_ref[...].reshape(1, chans), rgbw_ref[0:1, :], rgbw_ref[1:2, :], rgbw_ref[2:3, :])):
        prm[1 + q] = column(row)
    col = lax.broadcasted_iota(jnp.int32, (chans, L), 1)

    def shifted(prod, k, f, row):
        right = pltpu.roll(prod[:chans], 1, axis=1)
        left = pltpu.roll(prod[2 * chans :], L - 1, axis=1)
        done = None
        right_in = jnp.zeros((chans, L), F32)
        if k > 0:
            done = part[f, row] + jnp.where(col == L - 1, left, 0.0)
            right_in = edge[f, row]
        new = prod[chans : 2 * chans] + jnp.where(col == 0, right_in, right) + jnp.where(col == L - 1, 0.0, left)
        if k < n_chunks - 1:
            part[f, row] = new
            edge[f, row] = right
        return done, new

    def conv(p, k):
        buf = act if p == 0 else grad
        for f in range(2):
            for i in range(3):
                block = buf[k, f + i]
                if checks[p][f][i] is not None:
                    block = block * checks[p][f][i]
                rhs[k, i, :, :, f * L : (f + 1) * L] = block
        both = jnp.dot(w_mid[p], rhs[k].reshape(2 * tall, 2 * L), preferred_element_type=F32)
        above = jnp.dot(w_out[p, :tall], rhs[k, :, 0].reshape(tall, 2 * L), preferred_element_type=F32)
        below = jnp.dot(w_out[p, tall:], rhs[k, :, 1].reshape(tall, 2 * L), preferred_element_type=F32)
        for row, prod in enumerate((above, both[:tall], both[tall:], below)):
            for f in range(2):
                for q, value in zip((k - 1, k), shifted(prod[:, f * L : (f + 1) * L], k, f, row)):
                    if value is None or (q == k and k < n_chunks - 1):
                        continue
                    if row in (1, 2):
                        acc[q, f, row - 1] = value
                    else:
                        give[p, q, row // 3, f] = value.astype(BF16)
        if k > 0:
            send(p, k - 1, UP, DOWN)
        if k == n_chunks - 1:
            send(p, k, UP, DOWN)

    def xfloat(k, f, h):
        return fe[f, h, :, k * L : (k + 1) * L].astype(F32)

    def middle(k, f, h):
        yy = xfloat(k, f, h) + acc[k, f, h] + take[0, k, h, f].astype(F32)
        og = prm[1]
        ys = lax.rsqrt(jnp.mean(yy * yy, axis=0, keepdims=True) + EPS)
        yh = yy * ys
        yn = yh * og
        sg = jax.nn.sigmoid(yn)
        zz = yn * sg
        gz = jnp.zeros((chans, L), F32)
        for e in range(3):
            rgb = jnp.sum(prm[2 + e] * zz, axis=0, keepdims=True)
            d = jnp.clip(rgb - tgt[f, e, h : h + 1, k * L : (k + 1) * L], -DELTA, DELTA)
            gz = gz + prm[2 + e] * (pix[f, e, h : h + 1, k * L : (k + 1) * L] * d)
        v = gz * sg * (1.0 + yn * (1.0 - sg)) * og
        vp = jnp.mean(v * yh, axis=0, keepdims=True)
        g = ys * (v - yh * vp)
        gy[k, f, h] = g
        grad[k, f, h] = g.astype(BF16)

    def final(k, f, h, scale):
        ga = acc[k, f, h] + take[1, k, h, f].astype(F32)
        rs = rstd[k, f, h, 0:1, :]
        xh = xfloat(k, f, h) * rs
        u = ga * dterm[k, f, h]
        pj = jnp.mean(u * xh, axis=0, keepdims=True)
        res = (gy[k, f, h] + rs * (u - xh * pj)) * scale
        obuf[f, h, :, k * L : (k + 1) * L] = res.astype(BF16)

    def store(k):
        return pltpu.make_async_copy(
            obuf.at[:, :, :, pl.ds(k * L, L)], out_hbm.at[:, :, :, pl.ds(k * L, L)], osem.at[k]
        )

    cells = [(f, h) for f in range(2) for h in range(2)]

    for k in range(n_chunks):
        receive(0, k, Z)
        conv(0, k)
        if k in (1, 3):
            hailed(k // 2)
            hail(k // 2 + 1)
        if k == 3:
            sum_end(0)
            sum_start(1)

    prepare(1)
    for k in range(n_chunks):
        receive(0, k, UP, DOWN)
        for f, h in cells:
            middle(k, f, h)
        send(1, k, Z)

    sum_end(1)
    hailed(2)
    planes_start()

    for k in range(n_chunks):
        receive(1, k, Z)
        conv(1, k)
    scale = planes_end()
    for k in range(n_chunks):
        receive(1, k, UP, DOWN)
        for f, h in cells:
            final(k, f, h, scale)
        store(k).start()

    for p in range(2):
        for name, there in leaves[p].items():

            @pl.when(there)
            def _():
                for k in range(n_chunks):
                    copy(p, k, name).wait_send()

    for q in range(2):
        for c in sum_copies(q):
            c.wait_send()
    for d in reach:

        @pl.when(on_tm(d))
        def _():
            plane_copy(d).wait_send()

    for k in range(n_chunks):
        store(k).wait()


def local(feats, gain, conv_weight, out_gain, rgb_weight, target, pix_weight, frame_seg):
    n_tm, n_rows = lax.axis_size("tm"), lax.axis_size("rows")
    frames, rows, chans, width = feats.shape
    nc = width // L
    hbm = pl.BlockSpec(memory_space=pltpu.HBM)
    tall = 3 * chans
    return pl.pallas_call(
        functools.partial(kernel, n_tm, n_rows, 4, nc, chans),
        out_shape=pltpu.VMEM(feats.shape, BF16),
        in_specs=[hbm] * 8,
        out_specs=pl.BlockSpec(memory_space=pl.ANY),
        scratch_shapes=[
            pltpu.VMEM(feats.shape, BF16),
            pltpu.VMEM(gain.shape, F32),
            pltpu.VMEM(out_gain.shape, F32),
            pltpu.VMEM(rgb_weight.shape, F32),
            pltpu.SMEM(frame_seg.shape, jnp.int32),
            pltpu.VMEM((frames, 3, rows, width), F32),
            pltpu.VMEM((frames, 3, rows, width), F32),
            pltpu.VMEM(conv_weight.shape, BF16),
            pltpu.VMEM((2, 2 * tall, 2 * tall), BF16),
            pltpu.VMEM((2, 2 * tall, tall), BF16),
            pltpu.VMEM((nc, 3, rows, chans, 2 * L), BF16),
            pltpu.VMEM((5, chans, L), F32),
            pltpu.VMEM((nc, 4, 2, chans, L), BF16),
            pltpu.VMEM((nc, 4, 2, chans, L), BF16),
            pltpu.VMEM((nc, 2, 2, chans, L), F32),
            pltpu.VMEM((nc, 2, 2, 8, L), F32),
            pltpu.VMEM((nc, 2, 2, chans, L), F32),
            pltpu.VMEM((nc, 2, 2, chans, L), F32),
            pltpu.VMEM((2, 4, chans, L), F32),
            pltpu.VMEM((2, 4, chans, L), F32),
            pltpu.VMEM((2, nc, 2, 2, chans, L), BF16),
            pltpu.VMEM((2, nc, 2, 2, chans, L), BF16),
            pltpu.VMEM(feats.shape, BF16),
            pltpu.VMEM((3, 4, 1, L), F32),
            pltpu.VMEM((2 * n_tm - 1, 1, L), F32),
            pltpu.SemaphoreType.DMA((8,)),
            pltpu.SemaphoreType.DMA((nc,)),
            pltpu.SemaphoreType.DMA((2, nc, 3)),
            pltpu.SemaphoreType.DMA((2, nc, 3)),
            pltpu.SemaphoreType.DMA((2, 3)),
            pltpu.SemaphoreType.DMA((2, 3)),
            pltpu.SemaphoreType.DMA((2 * n_tm - 1,)),
            pltpu.SemaphoreType.DMA((2 * n_tm - 1,)),
            pltpu.SemaphoreType.REGULAR((3,)),
        ],
        compiler_params=pltpu.CompilerParams(
            collective_id=0, has_side_effects=True, vmem_limit_bytes=56 * 1024 * 1024
        ),
    )(
        feats, gain, conv_weight, out_gain, rgb_weight,
        target.transpose(0, 2, 1, 3), pix_weight.transpose(0, 2, 1, 3), frame_seg,
    )


def solution(mesh):
    placed = (
        P("tm", "rows", None, None),
        P(),
        P(),
        P(),
        P(),
        P("tm", "rows", None, None),
        P("tm", "rows", None, None),
        P(),
    )
    return jax.shard_map(
        local, mesh=mesh, in_specs=placed, out_specs=P("tm", "rows", None, None), check_vma=False
    )
```
